32 devices in a mesh: context: 4 (over z), head: 2 (over core), dp: 4 (over y, x).
Axes of the slice: x: 2, y: 2, z: 4, core: 2. Of those that a mesh axis runs over, the one named last changes fastest.
Arguments:
- lin_query: float32 [2048, 4096], P(('dp', 'context'), 'head'), parts along dimension 0, may hold values from -6 to 6
- lin_key: float32 [2048, 4096], P(('dp', 'context'), 'head'), parts along dimension 0, may hold values from -6 to 6
- lin_value: float32 [2048, 4096], P(('dp', 'context'), 'head'), parts along dimension 0, may hold values from -6 to 6
- lin_gate: float32 [2048, 4096], P(('dp', 'context'), 'head'), parts along dimension 0, may hold values from -8 to 8
- decay_rate: float32 [32, 2048], P('head', ('dp', 'context')), parts along dimension 1, may hold values from 0 to 1.5, as said below
- norm_gain: float32 [4096], P('head'), may hold values from 0.5 to 1.5
- sm_query: float32 [2048, 4096], P(('dp', 'context'), 'head'), parts along dimension 0, may hold values from -24 to 24
- sm_key: float32 [2048, 512], P(('dp', 'context'), 'head'), parts along dimension 0, may hold values from -24 to 24
- sm_value: float32 [2048, 512], P(('dp', 'context'), 'head'), parts along dimension 0, may hold values from -6 to 6
- doc_lengths: int32 [64], P('dp'), parts along dimension 0, may hold values from 1 to 384, 512 in all
Outputs:
- lin_out: float32 [2048, 4096], P(('dp', 'context'), 'head'), parts along dimension 0
- sm_out: float32 [2048, 4096], P(('dp', 'context'), 'head'), parts along dimension 0
The draws below stay inside these ranges and needn't reach their ends.
There are 4 independent parts, one for each index of `dp`. The reference program is written for one: setup_inputs(seed, part) draws one part's arguments, and reference() takes and returns one part's arrays. A program takes and returns all parts, laid end to end along the dimension named above; an argument that names none is the same for every part. Nothing has to cross between parts.
Inputs may be any that keep to these rules, and one draw needn't show every extreme that they name: `doc_lengths`: the 16 lengths sum to 512 and the longest is exactly 384. `decay_rate`: positive rates.
All inputs are finite; a program needn't handle non-finite values.
Results may differ from the reference program's by a relative error of at most 0.0003.
Values sent between devices are 32-bit elements; how exact they have to be, the bound alone decides.
A program may use at most 192 MiB of HBM per device.

```python
import math
import jax
import jax.numpy as jnp
import numpy as np
from jax import lax

ASKER_PLANES = 32
KV_HEADS = 4
HEAD_DIM = 128
ROT_DIM = 64
TOK_DEV = 128
DOCS = 16
SEQUENCE_SIZE = 512
MAXDOC = 384


def draw_decay_rate(key, part):
    matched_embeddings = jax.random.split(jax.random.fold_in(key, 3), 7)
    fast_share = 0.5
    fast = jax.random.uniform(matched_embeddings[0], (ASKER_PLANES, 1)) < fast_share
    fast_rate = jnp.exp(jax.random.uniform(matched_embeddings[1], (ASKER_PLANES, 1), minval=math.log(1.0 / 50.0), maxval=math.log(1.0 / 30.0)))
    slow_rate = jnp.exp(jax.random.uniform(matched_embeddings[2], (ASKER_PLANES, 1), minval=math.log(0.05), maxval=math.log(0.3))) / SEQUENCE_SIZE
    base_rate = jnp.where(fast, fast_rate, slow_rate)
    blocks = SEQUENCE_SIZE // TOK_DEV
    block_factor = jnp.exp(jax.random.uniform(matched_embeddings[3], (ASKER_PLANES, blocks, 1), minval=-0.7, maxval=0.7))
    token_factor = jnp.exp(jax.random.uniform(matched_embeddings[4], (ASKER_PLANES, blocks, TOK_DEV), minval=-0.3, maxval=0.3))
    forgetting_factors = (base_rate[:, :, None] * block_factor * token_factor).reshape(ASKER_PLANES, SEQUENCE_SIZE)
    segment_place = jax.random.randint(matched_embeddings[5], (ASKER_PLANES, 2), 0, SEQUENCE_SIZE)
    segment_extent = jax.random.uniform(matched_embeddings[6], (ASKER_PLANES, 2), minval=math.log(1.25), maxval=math.log(2.0))
    element_shift_number = jnp.arange(SEQUENCE_SIZE)[None, :]
    segment_ranges = jnp.where(element_shift_number == segment_place[:, 0:1], segment_extent[:, 0:1], 0.0) + jnp.where(element_shift_number == segment_place[:, 1:2], segment_extent[:, 1:2], 0.0)
    return (forgetting_factors + segment_ranges).astype(jnp.float32)


def base_values(key, shape):
    return jnp.clip(jax.random.normal(key, shape), -6.0, 6.0)


def draw_sm_key(key, part):
    base = base_values(jax.random.fold_in(key, 21), (SEQUENCE_SIZE, KV_HEADS, HEAD_DIM))
    return base.reshape(SEQUENCE_SIZE, KV_HEADS * HEAD_DIM).astype(jnp.float32)


def draw_sm_query(key, part):
    group = ASKER_PLANES // KV_HEADS
    base = base_values(jax.random.fold_in(key, 31), (SEQUENCE_SIZE, KV_HEADS, group, HEAD_DIM))
    return base.reshape(SEQUENCE_SIZE, ASKER_PLANES * HEAD_DIM).astype(jnp.float32)


def block_levels(rng, extent, cuts, smallest, high):
    gain = 1.0
    for position, parts in cuts:
        steps = jax.random.uniform(jax.random.fold_in(jax.random.fold_in(rng, 6), position), (parts,), jnp.float32, smallest / len(cuts), high / len(cuts))
        gain = gain * jnp.repeat(jnp.exp(steps), extent[position] // parts).reshape((-1,) + (1,) * (len(extent) - 1 - position))
    return gain


def length_profile(amount, total, most, lean):
    loads = [(1 << 20) // math.isqrt(standing ** lean) + 1 for standing in range(2, amount + 1)]
    spare, given = total - most - (amount - 1), [1] * (amount - 1)
    while spare > 0:
        candidates = [i for i in range(amount - 1) if given[i] < most]
        pool, left = sum([loads[i] for i in candidates]), spare
        for i in candidates:
            addition = min(most - given[i], max(1, left * loads[i] // pool), spare)
            given[i] = given[i] + addition
            spare = spare - addition
    return np.array([most] + given)


def uneven(key, count, total, bound, lean):
    if count == 2:
        one = jax.random.randint(key, (), max(1, total - bound), min(bound, total - 1) + 1)
        return jnp.stack([one, total - one])
    lengths = jnp.asarray(length_profile(count, total, bound, lean), jnp.int32)
    pairs = (count - 1) // 2
    giver, sink = lengths[1:1 + 2 * pairs:2], lengths[2:2 + 2 * pairs:2]
    room = jnp.minimum(giver - 1, bound - sink)
    shifted = jax.random.randint(jax.random.fold_in(key, 1), (pairs,), 0, 1 << 20) % (room + 1)
    lengths = lengths.at[1:1 + 2 * pairs:2].set(giver - shifted).at[2:2 + 2 * pairs:2].set(sink + shifted)
    return lengths[jax.random.permutation(jax.random.fold_in(key, 2), count)]


def scatter_about(stream_key, dims, scale, most, shards=(), kind=jnp.bfloat16):
    values = scale * jax.random.normal(stream_key, dims, jnp.float32)
    if shards:
        values = values * block_levels(stream_key, dims, shards, -0.22, 0.18)
    return jnp.clip(values, -most, most).astype(kind)


def setup_inputs(seed: int = 0, part: int = 0) -> dict:
    splits = jax.random.split(jax.random.key(seed), 11)
    part_splits = jax.random.split(jax.random.fold_in(splits[10], part), 11)
    return {
        "lin_query": scatter_about(part_splits[0], (SEQUENCE_SIZE, ASKER_PLANES * HEAD_DIM), 1.0, 6.0, ((0, 4), (1, 2)), jnp.float32),
        "lin_key": scatter_about(part_splits[1], (SEQUENCE_SIZE, ASKER_PLANES * HEAD_DIM), 1.0, 6.0, ((0, 4), (1, 2)), jnp.float32),
        "lin_value": scatter_about(part_splits[2], (SEQUENCE_SIZE, ASKER_PLANES * HEAD_DIM), 1.0, 6.0, ((0, 4), (1, 2)), jnp.float32),
        "lin_gate": scatter_about(part_splits[3], (SEQUENCE_SIZE, ASKER_PLANES * HEAD_DIM), 1.5, 8.0, ((0, 4), (1, 2)), jnp.float32),
        "decay_rate": draw_decay_rate(jax.random.fold_in(jax.random.fold_in(splits[10], part), 71), part),
        "norm_gain": jnp.clip(1.0 + 0.1 * jax.random.normal(splits[5], (ASKER_PLANES * HEAD_DIM,), jnp.float32), 0.5, 1.5),
        "sm_query": draw_sm_query(jax.random.fold_in(jax.random.fold_in(splits[10], part), 71), part),
        "sm_key": draw_sm_key(jax.random.fold_in(jax.random.fold_in(splits[10], part), 71), part),
        "sm_value": scatter_about(part_splits[8], (SEQUENCE_SIZE, KV_HEADS * HEAD_DIM), 1.0, 6.0, ((0, 4), (1, 2)), jnp.float32),
        "doc_lengths": uneven(part_splits[9], DOCS, SEQUENCE_SIZE, MAXDOC, 2).astype(jnp.int32),
    }


rope_base = 10000000.0
norm_eps = 1e-05
highest = lax.Precision.HIGHEST

def doc_tables(doc_lengths):
    doc_ends = jnp.cumsum(doc_lengths).astype(jnp.int32)
    doc_starts = (doc_ends - doc_lengths).astype(jnp.int32)
    return (doc_starts, doc_ends)

def doc_number(tokens_at, doc_ends):
    return lax.optimization_barrier(jnp.sum((doc_ends[None, :] <= tokens_at[:, None]).astype(jnp.int32), axis=1))

def doc_begin(tokens_at, doc_starts):
    picked = jnp.where(doc_starts[None, :] <= tokens_at[:, None], doc_starts[None, :], 0)
    return lax.optimization_barrier(jnp.max(picked, axis=1)).astype(jnp.int32)

def lightning_block(query_heads, key_heads, value_heads, forgetting_factors, first_token, doc_starts, doc_ends):
    width = query_heads.shape[1]
    tokens_at = first_token + jnp.arange(width, dtype=jnp.int32)
    doc_ids = doc_number(tokens_at, doc_ends)
    begins = doc_begin(tokens_at, doc_starts)
    log_decay = jnp.cumsum(-forgetting_factors, axis=1)
    visible = (doc_ids[:, None] == doc_ids[None, :]) & (tokens_at[:, None] >= tokens_at[None, :])
    spread = jnp.where(visible[None], log_decay[:, :, None] - log_decay[:, None, :], 0.0)
    weight = jnp.where(visible[None], jnp.exp(spread), 0.0)
    scores = jnp.einsum('htd,hsd->hts', query_heads, key_heads, precision=highest) * weight
    intra = jnp.einsum('hts,hsd->htd', scores, value_heads, precision=highest)
    carried_rows = begins < first_token
    block_decay = jnp.where(carried_rows[-1], jnp.exp(log_decay[:, -1]), 0.0)
    in_tail = doc_ids == doc_ids[-1]
    tail_gap = jnp.where(in_tail[None], log_decay[:, -1:] - log_decay, 0.0)
    tail_weight = jnp.where(in_tail[None], jnp.exp(tail_gap), 0.0)
    block_inner = jnp.einsum('htd,hte->hde', key_heads * tail_weight[:, :, None], value_heads, precision=highest)
    return (intra, log_decay, carried_rows, block_decay, block_inner)

def carried_term(query_heads, state, log_decay, carried_rows):
    reach_weight = jnp.where(carried_rows[None], jnp.exp(log_decay), 0.0)
    return jnp.einsum('htd,hde->hte', query_heads, state, precision=highest) * reach_weight[:, :, None]

def finish(attention, lin_gate, norm_gain):
    rows_count = attention.shape[0]
    per_head = attention.reshape(rows_count, -1, HEAD_DIM)
    mean_square = lax.optimization_barrier(jnp.mean(per_head * per_head, axis=-1, keepdims=True))
    normed = (per_head / jnp.sqrt(mean_square + norm_eps)).reshape(rows_count, -1)
    return normed * norm_gain[None, :] * jax.nn.sigmoid(lin_gate)

def rotate(heads_in, positions):
    half = ROT_DIM // 2
    inverse = rope_base ** (-(2.0 * jnp.arange(half, dtype=jnp.float32)) / ROT_DIM)
    angle = positions.astype(jnp.float32)[:, None] * inverse[None, :]
    cosine = jnp.cos(angle)[:, None, :]
    sine = jnp.sin(angle)[:, None, :]
    first_half = heads_in[..., :half]
    second_half = heads_in[..., half:ROT_DIM]
    return jnp.concatenate([first_half * cosine - second_half * sine, second_half * cosine + first_half * sine, heads_in[..., ROT_DIM:]], axis=-1)

def lightning(lin_query, lin_key, lin_value, decay_rate, doc_starts, doc_ends):
    blocks = SEQUENCE_SIZE // TOK_DEV

    def split_heads(matrix):
        return matrix.reshape(blocks, TOK_DEV, ASKER_PLANES, HEAD_DIM).transpose(0, 2, 1, 3)
    forgetting_factors = decay_rate.reshape(ASKER_PLANES, blocks, TOK_DEV).transpose(1, 0, 2)
    firsts = (jnp.arange(blocks, dtype=jnp.int32) * TOK_DEV).astype(jnp.int32)

    def advance(state, pieces):
        query_block, key_block, value_block, rate_block, first_token = pieces
        intra, log_decay, carried_rows, block_decay, block_inner = lightning_block(query_block, key_block, value_block, rate_block, first_token, doc_starts, doc_ends)
        result = intra + carried_term(query_block, state, log_decay, carried_rows)
        state = block_decay[:, None, None] * state + block_inner
        return (state, result)
    initial = jnp.zeros((ASKER_PLANES, HEAD_DIM, HEAD_DIM), jnp.float32)
    _, outputs = lax.scan(advance, initial, (split_heads(lin_query), split_heads(lin_key), split_heads(lin_value), forgetting_factors, firsts))
    return outputs.transpose(0, 2, 1, 3).reshape(SEQUENCE_SIZE, ASKER_PLANES * HEAD_DIM)

def softmax_layer(sm_query, sm_key, sm_value, doc_starts, doc_ends):
    group = ASKER_PLANES // KV_HEADS
    tokens_at = jnp.arange(SEQUENCE_SIZE, dtype=jnp.int32)
    positions = tokens_at - doc_begin(tokens_at, doc_starts)
    doc_ids = doc_number(tokens_at, doc_ends)
    queries = rotate(sm_query.reshape(SEQUENCE_SIZE, ASKER_PLANES, HEAD_DIM), positions)
    keys_all = rotate(sm_key.reshape(SEQUENCE_SIZE, KV_HEADS, HEAD_DIM), positions)
    values_all = sm_value.reshape(SEQUENCE_SIZE, KV_HEADS, HEAD_DIM)
    scale = HEAD_DIM ** (-0.5)
    blocks = SEQUENCE_SIZE // TOK_DEV

    def one_block(index):
        first_token = (index * TOK_DEV).astype(jnp.int32)
        query_rows = lax.dynamic_slice_in_dim(queries, first_token, TOK_DEV, 0).reshape(TOK_DEV, KV_HEADS, group, HEAD_DIM)
        rows_at = first_token + jnp.arange(TOK_DEV, dtype=jnp.int32)
        row_docs = lax.dynamic_slice_in_dim(doc_ids, first_token, TOK_DEV, 0)
        visible = (row_docs[:, None] == doc_ids[None, :]) & (rows_at[:, None] >= tokens_at[None, :])
        scores = jnp.einsum('tkgd,skd->kgts', query_rows, keys_all, precision=highest) * scale
        masked = jnp.where(visible[None, None], scores, -jnp.inf)
        top = lax.optimization_barrier(jnp.max(masked, axis=-1, keepdims=True))
        weights = jnp.where(visible[None, None], jnp.exp(masked - top), 0.0)
        total = lax.optimization_barrier(jnp.sum(weights, axis=-1))
        mixed = jnp.einsum('kgts,skd->kgtd', weights, values_all, precision=highest) / total[..., None]
        return mixed.transpose(2, 0, 1, 3).reshape(TOK_DEV, ASKER_PLANES * HEAD_DIM)
    outputs = lax.map(one_block, jnp.arange(blocks, dtype=jnp.int32))
    return outputs.reshape(SEQUENCE_SIZE, ASKER_PLANES * HEAD_DIM)

def reference(lin_query, lin_key, lin_value, lin_gate, decay_rate, norm_gain, sm_query, sm_key, sm_value, doc_lengths):
    doc_starts, doc_ends = doc_tables(doc_lengths)
    attention = lightning(lin_query, lin_key, lin_value, decay_rate, doc_starts, doc_ends)
    lin_out = finish(attention, lin_gate, norm_gain)
    sm_out = softmax_layer(sm_query, sm_key, sm_value, doc_starts, doc_ends)
    return (lin_out, sm_out)
```

```python
import functools

import jax
import jax.numpy as jnp
import numpy as np
from jax import lax
from jax.experimental import pallas as pl
from jax.experimental.pallas import tpu as pltpu
from jax.sharding import PartitionSpec as P

HEAD = 128
ROT = 64
BASE = 10000000.0
EPS = 1e-05
MESH = pl.DeviceIdType.MESH
HIGHEST = lax.Precision.HIGHEST
F32 = jnp.float32
BF16 = jnp.bfloat16
PAIR = 2


def rotary_tables(n, rows):
    half = ROT // 2
    exponent = -(2.0 * np.arange(half, dtype=np.float32)) / np.float32(ROT)
    inverse = np.power(np.float32(BASE), exponent.astype(np.float32)).astype(np.float64)
    place = np.arange(rows)[None, :] - rows * np.arange(n)[:, None]
    angle = place.reshape(-1, 1) * inverse[None, :]
    cosine = np.ones((n * rows, HEAD), np.float32)
    sine = np.zeros((n * rows, HEAD), np.float32)
    cosine[:, :half] = cosine[:, half:ROT] = np.cos(angle)
    sine[:, :half] = -np.sin(angle)
    sine[:, half:ROT] = np.sin(angle)
    return np.stack([cosine, sine])


def dot(a, b, contract, precision=None):
    return lax.dot_general(
        a, b, ((contract[0], contract[1]), ((), ())), precision=precision, preferred_element_type=F32
    )


def split(x):
    high = x.astype(BF16)
    return high, (x - high.astype(F32)).astype(BF16)


def rotated(x, cosine, sine):
    half = ROT // 2
    lane = lax.broadcasted_iota(jnp.int32, x.shape, 1)
    swapped = jnp.where(lane < half, pltpu.roll(x, HEAD - half, 1), pltpu.roll(x, half, 1))
    return x * cosine + swapped * sine


def kernel(
    n, rows, heads, kv, docs,
    len_ref, rate_ref, gain_ref, sk_hbm, sv_hbm, lk_hbm, lv_hbm, lq_hbm, sq_hbm, gate_hbm, tab_hbm,
    lin_hbm, sm_hbm,
    kvbuf, lk, lv, lq, sq, gate, tab, lin, sm, logd, begin, bias, keys, vals, inner, entered,
    load_sem, kv_send, kv_recv, st_send, st_recv, lin_sem, sm_sem,
):
    me = lax.axis_index("context")
    first = me * rows
    pairs = heads // PAIR
    group = heads // kv
    right = {"context": me + 1}

    loads = []
    for place, (src, dst) in enumerate(
        [
            (lk_hbm, lk), (lv_hbm, lv), (lq_hbm, lq), (sk_hbm, kvbuf.at[0, 0]), (sv_hbm, kvbuf.at[0, 1]),
            (tab_hbm, tab), (sq_hbm, sq), (gate_hbm, gate),
        ]
    ):
        copy = pltpu.make_async_copy(src, dst, load_sem.at[place])
        copy.start()
        loads.append(copy)

    def kv_copy(slot, which):
        src = (sk_hbm, sv_hbm)[which] if slot == 0 else kvbuf.at[slot, which]
        return pltpu.make_async_remote_copy(
            src_ref=src, dst_ref=kvbuf.at[slot + 1, which],
            send_sem=kv_send.at[slot, which], recv_sem=kv_recv.at[slot + 1, which],
            device_id=right, device_id_type=MESH,
        )

    def kv_arrival(slot, which):
        return pltpu.make_async_remote_copy(
            src_ref=kvbuf.at[slot, which], dst_ref=kvbuf.at[slot, which],
            send_sem=kv_send.at[slot, which], recv_sem=kv_recv.at[slot, which],
            device_id=right, device_id_type=MESH,
        )

    def state_copy(pair):
        here = pl.ds(pair * PAIR, PAIR)
        return pltpu.make_async_remote_copy(
            src_ref=inner.at[here], dst_ref=entered.at[here],
            send_sem=st_send.at[pair], recv_sem=st_recv.at[pair],
            device_id=right, device_id_type=MESH,
        )

    barrier = pltpu.get_barrier_semaphore()

    @pl.when(me > 0)
    def _():
        pl.semaphore_signal(barrier, inc=1, device_id={"context": me - 1}, device_id_type=MESH)

    @pl.when(me < n - 1)
    def _():
        pl.semaphore_wait(barrier, 1)
        kv_copy(0, 0).start()
        kv_copy(0, 1).start()

    row = first + lax.broadcasted_iota(jnp.int32, (rows, rows), 0)
    lane = lax.broadcasted_iota(jnp.int32, (rows, rows), 1)
    last = first + rows - 1
    start = jnp.int32(0)
    starts = jnp.zeros((rows, rows), jnp.int32)
    start_last = jnp.int32(0)
    for d in range(docs):
        starts = jnp.where(row >= start, start, starts)
        start_last = jnp.where(last >= start, start, start_last)
        start = start + len_ref[d]
    begin[...] = starts
    for slot in range(n):
        column = rows * (me - slot) + lane
        bias[:, slot * rows:(slot + 1) * rows] = jnp.where(
            (column >= starts) & (column <= row), 0.0, -jnp.inf
        ).astype(F32)
    upper = jnp.where(
        lax.broadcasted_iota(jnp.int32, (rows, rows), 0) <= lane, 1.0, 0.0
    ).astype(F32)
    logd[...] = dot(-rate_ref[...], upper, ((1,), (0,)), HIGHEST)

    def lanes(head):
        return pl.ds(pl.multiple_of(head * HEAD, HEAD), HEAD)

    def log_rows(head):
        one = logd[pl.ds(head, 1), :]
        return (
            jnp.broadcast_to(one, (rows, rows)),
            jnp.broadcast_to(one[:, rows - 1:], (rows, rows)),
        )

    loads[0].wait()
    loads[1].wait()
    in_tail = first + lane >= start_last

    def inner_pair(pair, _):
        for j in range(PAIR):
            head = pair * PAIR + j
            along, end = log_rows(head)
            weight = jnp.exp(jnp.where(in_tail, end - along, -jnp.inf))
            turned = lk[:, lanes(head)].T * weight
            inner[head] = dot(turned, lv[:, lanes(head)], ((1,), (0,)), HIGHEST)

        @pl.when(me == 0)
        def _():
            if n > 1:
                state_copy(pair).start()

        return 0

    lax.fori_loop(0, pairs, inner_pair, 0)

    def place_keys(slot):
        at = slice(slot * rows, (slot + 1) * rows)
        cosine, sine = tab[0, at, :], tab[1, at, :]
        for g in range(kv):
            features = slice(g * HEAD, (g + 1) * HEAD)
            high, low = split(rotated(kvbuf[slot, 0, :, features], cosine, sine))
            keys[g, at, :] = jnp.concatenate([high, high], axis=1)
            keys[g, n * rows + slot * rows:n * rows + (slot + 1) * rows, :] = jnp.concatenate(
                [low, low], axis=1
            )
            high, low = split(kvbuf[slot, 1, :, features])
            both = jnp.concatenate([high, low], axis=1)
            vals[g, at, :] = both
            vals[g, n * rows + slot * rows:n * rows + (slot + 1) * rows, :] = both

    def receive(slot):
        @pl.when(me >= slot)
        def _():
            for which in range(2):
                kv_arrival(slot, which).wait_recv()
                if slot < n - 1:
                    @pl.when(me < n - 1)
                    def _():
                        kv_copy(slot, which).start()
            place_keys(slot)

        @pl.when(me < slot)
        def _():
            for g in range(kv):
                for base in (0, n * rows):
                    at = slice(base + slot * rows, base + (slot + 1) * rows)
                    keys[g, at, :] = jnp.zeros((rows, 2 * HEAD), BF16)
                    vals[g, at, :] = jnp.zeros((rows, 2 * HEAD), BF16)

    loads[2].wait()
    for copy in loads[3:6]:
        copy.wait()
    if n > 1:
        receive(1)
    place_keys(0)

    def intra_pair(pair, _):
        visible = bias[:, 0:rows] == 0.0
        carried = begin[...] < first
        for j in range(PAIR):
            head = pair * PAIR + j
            along, _end = log_rows(head)
            down = along.T
            weight = jnp.exp(jnp.where(visible, down - along, -jnp.inf))
            query = lq[:, lanes(head)]
            scores = dot(query, lk[:, lanes(head)], ((1,), (1,)), HIGHEST) * weight
            lin[:, lanes(head)] = dot(scores, lv[:, lanes(head)], ((1,), (0,)), HIGHEST)
            reach = jnp.exp(jnp.where(carried, down, -jnp.inf))
            lq[:, lanes(head)] = query * reach
        return 0

    lax.fori_loop(0, pairs, intra_pair, 0)
    for slot in range(2, n):
        receive(slot)

    loads[6].wait()
    loads[7].wait()

    @pl.when(me == 0)
    def _():
        entered[...] = jnp.zeros_like(entered)

    scale = HEAD ** -0.5

    def finish_pair(pair, _):
        @pl.when(me > 0)
        def _():
            state_copy(pair).wait_recv()

        for j in range(PAIR):
            head = pair * PAIR + j
            _along, end = log_rows(head)
            decay = jnp.exp(jnp.where(start_last < first, end, -jnp.inf))
            inner_out = decay * entered[head]

            @pl.when(me > 0)
            def _():
                inner[head] = inner[head] + inner_out

        @pl.when((me > 0) & (me < n - 1))
        def _():
            state_copy(pair).start()

        queries = []
        for j in range(PAIR):
            head = pair * PAIR + j
            attention = lin[:, lanes(head)] + dot(
                lq[:, lanes(head)], entered[head], ((1,), (0,)), HIGHEST
            )
            square = jnp.mean(attention * attention, axis=1, keepdims=True)
            normed = attention * lax.rsqrt(square + EPS) * gain_ref[:, lanes(head)]
            lin[:, lanes(head)] = normed / (1.0 + jnp.exp(-gate[:, lanes(head)]))
            turned = rotated(sq[:, lanes(head)], tab[0, 0:rows, :], tab[1, 0:rows, :]) * scale
            queries.append(jnp.concatenate(split(turned), axis=1))
        query = jnp.concatenate(queries, axis=0)
        g = lax.div(pair * PAIR, group)
        width = n * rows
        products = dot(query, keys[g], ((1,), (1,)))
        scores = products[:, :width] + products[:, width:]
        scores = scores + jnp.concatenate([bias[...]] * PAIR, axis=0)
        weights = jnp.exp(scores - jnp.max(scores, axis=1, keepdims=True))
        total = jnp.sum(weights, axis=1, keepdims=True)
        mixed = dot(jnp.concatenate(split(weights), axis=1), vals[g], ((1,), (0,)))
        mixed = (mixed[:, :HEAD] + mixed[:, HEAD:]) / total
        for j in range(PAIR):
            sm[:, lanes(pair * PAIR + j)] = mixed[j * rows:(j + 1) * rows]
        out_copy(lin, lin_hbm, lin_sem, pair).start()
        out_copy(sm, sm_hbm, sm_sem, pair).start()
        return 0

    def out_copy(src, dst, sem, pair):
        at = pl.ds(pl.multiple_of(pair * PAIR * HEAD, PAIR * HEAD), PAIR * HEAD)
        return pltpu.make_async_copy(src.at[:, at], dst.at[:, at], sem.at[pair])

    lax.fori_loop(0, pairs, finish_pair, 0)

    def drain(pair, _):
        out_copy(lin, lin_hbm, lin_sem, pair).wait()
        out_copy(sm, sm_hbm, sm_sem, pair).wait()

        @pl.when(me < n - 1)
        def _():
            state_copy(pair).wait_send()

        return 0

    lax.fori_loop(0, pairs, drain, 0)
    for slot in range(n - 1):
        @pl.when((me < n - 1) & (me >= slot))
        def _():
            kv_copy(slot, 0).wait_send()
            kv_copy(slot, 1).wait_send()


def shards(
    n, lin_query, lin_key, lin_value, lin_gate, decay_rate, norm_gain, sm_query, sm_key, sm_value, doc_lengths
):
    rows, features = lin_query.shape
    heads, kv = features // HEAD, sm_key.shape[1] // HEAD
    docs = doc_lengths.shape[0]
    pairs = heads // PAIR
    width = n * rows
    vmem = pl.BlockSpec(memory_space=pltpu.VMEM)
    anywhere = pl.BlockSpec(memory_space=pl.ANY)
    big = pltpu.VMEM((rows, features), F32)
    table = jnp.asarray(rotary_tables(n, rows))
    out = jax.ShapeDtypeStruct((rows, features), F32)
    call = pl.pallas_call(
        functools.partial(kernel, n, rows, heads, kv, docs),
        out_shape=(out, out),
        in_specs=[pl.BlockSpec(memory_space=pltpu.SMEM), vmem, vmem] + [anywhere] * 8,
        out_specs=(anywhere, anywhere),
        scratch_shapes=[
            pltpu.VMEM((n, 2, rows, kv * HEAD), F32),
            big, big, big, big, big,
            pltpu.VMEM((2, width, HEAD), F32),
            big, big,
            pltpu.VMEM((heads, rows), F32),
            pltpu.VMEM((rows, rows), jnp.int32),
            pltpu.VMEM((rows, width), F32),
            pltpu.VMEM((kv, 2 * width, 2 * HEAD), BF16),
            pltpu.VMEM((kv, 2 * width, 2 * HEAD), BF16),
            pltpu.VMEM((heads, HEAD, HEAD), F32),
            pltpu.VMEM((heads, HEAD, HEAD), F32),
            pltpu.SemaphoreType.DMA((8,)),
            pltpu.SemaphoreType.DMA((n, 2)),
            pltpu.SemaphoreType.DMA((n, 2)),
            pltpu.SemaphoreType.DMA((pairs,)),
            pltpu.SemaphoreType.DMA((pairs,)),
            pltpu.SemaphoreType.DMA((pairs,)),
            pltpu.SemaphoreType.DMA((pairs,)),
        ],
        compiler_params=pltpu.CompilerParams(
            collective_id=0, has_side_effects=True, vmem_limit_bytes=60 * 1024 * 1024
        ),
    )
    return call(
        doc_lengths, decay_rate, norm_gain.reshape(1, features), sm_key, sm_value,
        lin_key, lin_value, lin_query, sm_query, lin_gate, table,
    )


def solution(mesh):
    tokens = P(("dp", "context"), "head")
    in_specs = (
        tokens, tokens, tokens, tokens, P("head", ("dp", "context")), P("head"),
        tokens, tokens, tokens, P("dp"),
    )
    return jax.shard_map(
        functools.partial(shards, mesh.shape["context"]),
        mesh=mesh, in_specs=in_specs, out_specs=(tokens, tokens), check_vma=False,
    )
```

```python
import functools

import jax
import jax.numpy as jnp
import numpy as np
from jax import lax
from jax.experimental import pallas as pl
from jax.experimental.pallas import tpu as pltpu
from jax.sharding import PartitionSpec as P

HEAD = 128
ROT = 64
BASE = 10000000.0
EPS = 1e-05
MESH = pl.DeviceIdType.MESH
HIGHEST = lax.Precision.HIGHEST
F32 = jnp.float32
BF16 = jnp.bfloat16
PAIR = 2


def rotary_tables(n, rows):
    half = ROT // 2
    exponent = -(2.0 * np.arange(half, dtype=np.float32)) / np.float32(ROT)
    inverse = np.power(np.float32(BASE), exponent.astype(np.float32)).astype(np.float64)
    place = np.arange(rows)[None, :] - rows * np.arange(n)[:, None]
    angle = place.reshape(-1, 1) * inverse[None, :]
    cosine = np.ones((n * rows, HEAD), np.float32)
    sine = np.zeros((n * rows, HEAD), np.float32)
    cosine[:, :half] = cosine[:, half:ROT] = np.cos(angle)
    sine[:, :half] = -np.sin(angle)
    sine[:, half:ROT] = np.sin(angle)
    return np.stack([cosine, sine])


def dot(a, b, contract, precision=None):
    return lax.dot_general(
        a, b, ((contract[0], contract[1]), ((), ())), precision=precision, preferred_element_type=F32
    )


def split(x):
    high = x.astype(BF16)
    return high, (x - high.astype(F32)).astype(BF16)


def halves(x):
    return jnp.concatenate(split(x), axis=1)


def against_rows(lhs, rhs):
    high, low = split(rhs)
    wide = jnp.concatenate(
        [jnp.concatenate([high, high], axis=1), jnp.concatenate([low, low], axis=1)], axis=0
    )
    out = dot(lhs, wide, ((1,), (1,)))
    return out[:, :HEAD] + out[:, HEAD:]


def against_columns(lhs, rhs):
    out = dot(lhs, jnp.concatenate([rhs, rhs], axis=0), ((1,), (0,)))
    return out[:, :HEAD] + out[:, HEAD:]


def rotated(x, cosine, sine):
    half = ROT // 2
    lane = lax.broadcasted_iota(jnp.int32, x.shape, 1)
    swapped = jnp.where(lane < half, pltpu.roll(x, HEAD - half, 1), pltpu.roll(x, half, 1))
    return x * cosine + swapped * sine


def kernel(
    n, rows, heads, kv, docs,
    len_ref, rate_ref, gain_ref, sk_hbm, sv_hbm, lk_hbm, lv_hbm, lq_hbm, sq_hbm, gate_hbm, tab_hbm,
    lin_hbm, sm_hbm,
    kvbuf, lk, lv, lq, sq, gate, tab, lin, sm, logd, begin, bias, keys, vals, lvh, lqh, inner, entered,
    load_sem, kv_send, kv_recv, st_send, st_recv, lin_sem, sm_sem,
):
    me = lax.axis_index("context")
    first = me * rows
    pairs = heads // PAIR
    group = heads // kv
    right = {"context": me + 1}

    loads = []
    for place, (src, dst) in enumerate(
        [
            (lk_hbm, lk), (lv_hbm, lv), (lq_hbm, lq), (sk_hbm, kvbuf.at[0, 0]), (sv_hbm, kvbuf.at[0, 1]),
            (tab_hbm, tab), (sq_hbm, sq), (gate_hbm, gate),
        ]
    ):
        copy = pltpu.make_async_copy(src, dst, load_sem.at[place])
        copy.start()
        loads.append(copy)

    def kv_copy(slot, which):
        src = (sk_hbm, sv_hbm)[which] if slot == 0 else kvbuf.at[slot, which]
        return pltpu.make_async_remote_copy(
            src_ref=src, dst_ref=kvbuf.at[slot + 1, which],
            send_sem=kv_send.at[slot, which], recv_sem=kv_recv.at[slot + 1, which],
            device_id=right, device_id_type=MESH,
        )

    def kv_arrival(slot, which):
        return pltpu.make_async_remote_copy(
            src_ref=kvbuf.at[slot, which], dst_ref=kvbuf.at[slot, which],
            send_sem=kv_send.at[slot, which], recv_sem=kv_recv.at[slot, which],
            device_id=right, device_id_type=MESH,
        )

    def state_copy(pair):
        here = pl.ds(pair * PAIR, PAIR)
        return pltpu.make_async_remote_copy(
            src_ref=inner.at[here], dst_ref=entered.at[here],
            send_sem=st_send.at[pair], recv_sem=st_recv.at[pair],
            device_id=right, device_id_type=MESH,
        )

    barrier = pltpu.get_barrier_semaphore()

    @pl.when(me > 0)
    def _():
        pl.semaphore_signal(barrier, inc=1, device_id={"context": me - 1}, device_id_type=MESH)

    @pl.when(me < n - 1)
    def _():
        pl.semaphore_wait(barrier, 1)
        kv_copy(0, 0).start()
        kv_copy(0, 1).start()

    row = first + lax.broadcasted_iota(jnp.int32, (rows, rows), 0)
    lane = lax.broadcasted_iota(jnp.int32, (rows, rows), 1)
    last = first + rows - 1
    start = jnp.int32(0)
    starts = jnp.zeros((rows, rows), jnp.int32)
    start_last = jnp.int32(0)
    for d in range(docs):
        starts = jnp.where(row >= start, start, starts)
        start_last = jnp.where(last >= start, start, start_last)
        start = start + len_ref[d]
    begin[...] = starts
    for slot in range(n):
        column = rows * (me - slot) + lane
        bias[:, slot * rows:(slot + 1) * rows] = jnp.where(
            (column >= starts) & (column <= row), 0.0, -jnp.inf
        ).astype(F32)
    upper = jnp.where(
        lax.broadcasted_iota(jnp.int32, (rows, rows), 0) <= lane, 1.0, 0.0
    ).astype(F32)
    logd[...] = dot(-rate_ref[...], upper, ((1,), (0,)), HIGHEST)

    def lanes(head):
        return pl.ds(pl.multiple_of(head * HEAD, HEAD), HEAD)

    def log_rows(head):
        one = logd[pl.ds(head, 1), :]
        return (
            jnp.broadcast_to(one, (rows, rows)),
            jnp.broadcast_to(one[:, rows - 1:], (rows, rows)),
        )

    loads[0].wait()
    loads[1].wait()
    in_tail = first + lane >= start_last

    def inner_pair(pair, _):
        for j in range(PAIR):
            head = pair * PAIR + j
            along, end = log_rows(head)
            weight = jnp.exp(jnp.where(in_tail, end - along, -jnp.inf))
            turned = lk[:, lanes(head)].T * weight
            both = halves(lv[:, lanes(head)])
            lvh[head] = both
            inner[head] = against_columns(halves(turned), both)

        @pl.when(me == 0)
        def _():
            if n > 1:
                state_copy(pair).start()

        return 0

    lax.fori_loop(0, pairs, inner_pair, 0)

    def place_keys(slot):
        at = slice(slot * rows, (slot + 1) * rows)
        cosine, sine = tab[0, at, :], tab[1, at, :]
        for g in range(kv):
            features = slice(g * HEAD, (g + 1) * HEAD)
            high, low = split(rotated(kvbuf[slot, 0, :, features], cosine, sine))
            keys[g, at, :] = jnp.concatenate([high, high], axis=1)
            keys[g, n * rows + slot * rows:n * rows + (slot + 1) * rows, :] = jnp.concatenate(
                [low, low], axis=1
            )
            high, low = split(kvbuf[slot, 1, :, features])
            both = jnp.concatenate([high, low], axis=1)
            vals[g, at, :] = both
            vals[g, n * rows + slot * rows:n * rows + (slot + 1) * rows, :] = both

    def receive(slot):
        @pl.when(me >= slot)
        def _():
            for which in range(2):
                kv_arrival(slot, which).wait_recv()
                if slot < n - 1:
                    @pl.when(me < n - 1)
                    def _():
                        kv_copy(slot, which).start()
            place_keys(slot)

        @pl.when(me < slot)
        def _():
            for g in range(kv):
                for base in (0, n * rows):
                    at = slice(base + slot * rows, base + (slot + 1) * rows)
                    keys[g, at, :] = jnp.zeros((rows, 2 * HEAD), BF16)
                    vals[g, at, :] = jnp.zeros((rows, 2 * HEAD), BF16)

    loads[2].wait()
    for copy in loads[3:6]:
        copy.wait()
    if n > 1:
        receive(1)
    place_keys(0)

    def intra_pair(pair, _):
        visible = bias[:, 0:rows] == 0.0
        carried = begin[...] < first
        for j in range(PAIR):
            head = pair * PAIR + j
            along, _end = log_rows(head)
            down = along.T
            weight = jnp.exp(jnp.where(visible, down - along, -jnp.inf))
            query = lq[:, lanes(head)]
            scores = against_rows(halves(query), lk[:, lanes(head)]) * weight
            lin[:, lanes(head)] = against_columns(halves(scores), lvh[head])
            reach = jnp.exp(jnp.where(carried, down, -jnp.inf))
            lqh[head] = halves(query * reach)
        return 0

    lax.fori_loop(0, pairs, intra_pair, 0)
    for slot in range(2, n):
        receive(slot)

    loads[6].wait()
    loads[7].wait()

    @pl.when(me == 0)
    def _():
        entered[...] = jnp.zeros_like(entered)

    scale = HEAD ** -0.5

    def finish_pair(pair, _):
        @pl.when(me > 0)
        def _():
            state_copy(pair).wait_recv()

        for j in range(PAIR):
            head = pair * PAIR + j
            _along, end = log_rows(head)
            decay = jnp.exp(jnp.where(start_last < first, end, -jnp.inf))
            inner_out = decay * entered[head]

            @pl.when(me > 0)
            def _():
                inner[head] = inner[head] + inner_out

        @pl.when((me > 0) & (me < n - 1))
        def _():
            state_copy(pair).start()

        queries = []
        for j in range(PAIR):
            head = pair * PAIR + j
            attention = lin[:, lanes(head)] + against_columns(lqh[head], halves(entered[head]))
            square = jnp.mean(attention * attention, axis=1, keepdims=True)
            normed = attention * lax.rsqrt(square + EPS) * gain_ref[:, lanes(head)]
            lin[:, lanes(head)] = normed / (1.0 + jnp.exp(-gate[:, lanes(head)]))
            turned = rotated(sq[:, lanes(head)], tab[0, 0:rows, :], tab[1, 0:rows, :]) * scale
            queries.append(jnp.concatenate(split(turned), axis=1))
        query = jnp.concatenate(queries, axis=0)
        g = lax.div(pair * PAIR, group)
        width = n * rows
        products = dot(query, keys[g], ((1,), (1,)))
        scores = products[:, :width] + products[:, width:]
        scores = scores + jnp.concatenate([bias[...]] * PAIR, axis=0)
        weights = jnp.exp(scores - jnp.max(scores, axis=1, keepdims=True))
        total = jnp.sum(weights, axis=1, keepdims=True)
        mixed = dot(jnp.concatenate(split(weights), axis=1), vals[g], ((1,), (0,)))
        mixed = (mixed[:, :HEAD] + mixed[:, HEAD:]) / total
        for j in range(PAIR):
            sm[:, lanes(pair * PAIR + j)] = mixed[j * rows:(j + 1) * rows]
        out_copy(lin, lin_hbm, lin_sem, pair).start()
        out_copy(sm, sm_hbm, sm_sem, pair).start()
        return 0

    def out_copy(src, dst, sem, pair):
        at = pl.ds(pl.multiple_of(pair * PAIR * HEAD, PAIR * HEAD), PAIR * HEAD)
        return pltpu.make_async_copy(src.at[:, at], dst.at[:, at], sem.at[pair])

    lax.fori_loop(0, pairs, finish_pair, 0)

    def drain(pair, _):
        out_copy(lin, lin_hbm, lin_sem, pair).wait()
        out_copy(sm, sm_hbm, sm_sem, pair).wait()

        @pl.when(me < n - 1)
        def _():
            state_copy(pair).wait_send()

        return 0

    lax.fori_loop(0, pairs, drain, 0)
    for slot in range(n - 1):
        @pl.when((me < n - 1) & (me >= slot))
        def _():
            kv_copy(slot, 0).wait_send()
            kv_copy(slot, 1).wait_send()


def shards(
    n, lin_query, lin_key, lin_value, lin_gate, decay_rate, norm_gain, sm_query, sm_key, sm_value, doc_lengths
):
    rows, features = lin_query.shape
    heads, kv = features // HEAD, sm_key.shape[1] // HEAD
    docs = doc_lengths.shape[0]
    pairs = heads // PAIR
    width = n * rows
    vmem = pl.BlockSpec(memory_space=pltpu.VMEM)
    anywhere = pl.BlockSpec(memory_space=pl.ANY)
    big = pltpu.VMEM((rows, features), F32)
    table = jnp.asarray(rotary_tables(n, rows))
    out = jax.ShapeDtypeStruct((rows, features), F32)
    call = pl.pallas_call(
        functools.partial(kernel, n, rows, heads, kv, docs),
        out_shape=(out, out),
        in_specs=[pl.BlockSpec(memory_space=pltpu.SMEM), vmem, vmem] + [anywhere] * 8,
        out_specs=(anywhere, anywhere),
        scratch_shapes=[
            pltpu.VMEM((n, 2, rows, kv * HEAD), F32),
            big, big, big, big, big,
            pltpu.VMEM((2, width, HEAD), F32),
            big, big,
            pltpu.VMEM((heads, rows), F32),
            pltpu.VMEM((rows, rows), jnp.int32),
            pltpu.VMEM((rows, width), F32),
            pltpu.VMEM((kv, 2 * width, 2 * HEAD), BF16),
            pltpu.VMEM((kv, 2 * width, 2 * HEAD), BF16),
            pltpu.VMEM((heads, rows, 2 * HEAD), BF16),
            pltpu.VMEM((heads, rows, 2 * HEAD), BF16),
            pltpu.VMEM((heads, HEAD, HEAD), F32),
            pltpu.VMEM((heads, HEAD, HEAD), F32),
            pltpu.SemaphoreType.DMA((8,)),
            pltpu.SemaphoreType.DMA((n, 2)),
            pltpu.SemaphoreType.DMA((n, 2)),
            pltpu.SemaphoreType.DMA((pairs,)),
            pltpu.SemaphoreType.DMA((pairs,)),
            pltpu.SemaphoreType.DMA((pairs,)),
            pltpu.SemaphoreType.DMA((pairs,)),
        ],
        compiler_params=pltpu.CompilerParams(
            collective_id=0, has_side_effects=True, vmem_limit_bytes=60 * 1024 * 1024
        ),
    )
    return call(
        doc_lengths, decay_rate, norm_gain.reshape(1, features), sm_key, sm_value,
        lin_key, lin_value, lin_query, sm_query, lin_gate, table,
    )


def solution(mesh):
    tokens = P(("dp", "context"), "head")
    in_specs = (
        tokens, tokens, tokens, tokens, P("head", ("dp", "context")), P("head"),
        tokens, tokens, tokens, P("dp"),
    )
    return jax.shard_map(
        functools.partial(shards, mesh.shape["context"]),
        mesh=mesh, in_specs=in_specs, out_specs=(tokens, tokens), check_vma=False,
    )
```

```python
import functools

import jax
import jax.numpy as jnp
import numpy as np
from jax import lax
from jax.experimental import pallas as pl
from jax.experimental.pallas import tpu as pltpu
from jax.sharding import PartitionSpec as P

HEAD = 128
ROT = 64
BASE = 10000000.0
EPS = 1e-05
MESH = pl.DeviceIdType.MESH
HIGHEST = lax.Precision.HIGHEST
F32 = jnp.float32
BF16 = jnp.bfloat16
PAIR = 2
PARTS = 4


def rotary_tables(n, rows):
    half = ROT // 2
    exponent = -(2.0 * np.arange(half, dtype=np.float32)) / np.float32(ROT)
    inverse = np.power(np.float32(BASE), exponent.astype(np.float32)).astype(np.float64)
    place = np.arange(rows)[None, :] - rows * np.arange(n)[:, None]
    angle = place.reshape(-1, 1) * inverse[None, :]
    cosine = np.ones((n * rows, HEAD), np.float32)
    sine = np.zeros((n * rows, HEAD), np.float32)
    cosine[:, :half] = cosine[:, half:ROT] = np.cos(angle)
    sine[:, :half] = -np.sin(angle)
    sine[:, half:ROT] = np.sin(angle)
    return np.stack([cosine, sine])


def dot(a, b, contract, precision=None):
    return lax.dot_general(
        a, b, ((contract[0], contract[1]), ((), ())), precision=precision, preferred_element_type=F32
    )


def split(x):
    high = x.astype(BF16)
    return high, (x - high.astype(F32)).astype(BF16)


def halves(x):
    return jnp.concatenate(split(x), axis=1)


def against_rows(lhs, rhs):
    high, low = split(rhs)
    wide = jnp.concatenate(
        [jnp.concatenate([high, high], axis=1), jnp.concatenate([low, low], axis=1)], axis=0
    )
    out = dot(lhs, wide, ((1,), (1,)))
    return out[:, :HEAD] + out[:, HEAD:]


def against_columns(lhs, rhs):
    out = dot(lhs, jnp.concatenate([rhs, rhs], axis=0), ((1,), (0,)))
    return out[:, :HEAD] + out[:, HEAD:]


def rotated(x, cosine, sine):
    half = ROT // 2
    lane = lax.broadcasted_iota(jnp.int32, x.shape, 1)
    swapped = jnp.where(lane < half, pltpu.roll(x, HEAD - half, 1), pltpu.roll(x, half, 1))
    return x * cosine + swapped * sine


def kernel(
    n, rows, heads, kv, docs,
    len_ref, rate_hbm, gain_hbm, sk_hbm, sv_hbm, lk_hbm, lv_hbm, lq_hbm, sq_hbm, gate_hbm, tab_hbm,
    lin_hbm, sm_hbm,
    rate_ref, gain_ref, kvbuf, lk, lv, lq, sq, gate, tab, lin, sm, logd, begin, bias, keys, vals, lvh, lqh, inner, entered,
    load_sem, kv_send, kv_recv, st_send, st_recv, lin_sem, sm_sem,
):
    me = lax.axis_index("context")
    first = me * rows
    pairs = heads // PAIR
    group = heads // kv
    right = {"context": me + 1}

    barrier = pltpu.get_barrier_semaphore()

    @pl.when(me > 0)
    def _():
        pl.semaphore_signal(barrier, inc=1, device_id={"context": me - 1}, device_id_type=MESH)

    loads = [
        pltpu.make_async_copy(src, dst, load_sem.at[place])
        for place, (src, dst) in enumerate(
            [
                (rate_hbm, rate_ref), (lk_hbm, lk), (lv_hbm, lv), (sk_hbm, kvbuf.at[0, 0]),
                (sv_hbm, kvbuf.at[0, 1]), (tab_hbm, tab), (lq_hbm, lq), (sq_hbm, sq), (gate_hbm, gate),
                (gain_hbm, gain_ref),
            ]
        )
    ]
    for copy in loads[:3]:
        copy.start()

    def kv_copy(slot, which):
        src = (sk_hbm, sv_hbm)[which] if slot == 0 else kvbuf.at[slot, which]
        return pltpu.make_async_remote_copy(
            src_ref=src, dst_ref=kvbuf.at[slot + 1, which],
            send_sem=kv_send.at[slot, which], recv_sem=kv_recv.at[slot + 1, which],
            device_id=right, device_id_type=MESH,
        )

    def kv_arrival(slot, which):
        return pltpu.make_async_remote_copy(
            src_ref=kvbuf.at[slot, which], dst_ref=kvbuf.at[slot, which],
            send_sem=kv_send.at[slot, which], recv_sem=kv_recv.at[slot, which],
            device_id=right, device_id_type=MESH,
        )

    def state_copy(pair):
        here = pl.ds(pair * PAIR, PAIR)
        return pltpu.make_async_remote_copy(
            src_ref=inner.at[here], dst_ref=entered.at[here],
            send_sem=st_send.at[pair], recv_sem=st_recv.at[pair],
            device_id=right, device_id_type=MESH,
        )

    @pl.when(me < n - 1)
    def _():
        pl.semaphore_wait(barrier, 1)
        kv_copy(0, 0).start()
        kv_copy(0, 1).start()

    for copy in loads[3:]:
        copy.start()

    row = first + lax.broadcasted_iota(jnp.int32, (rows, rows), 0)
    lane = lax.broadcasted_iota(jnp.int32, (rows, rows), 1)
    last = first + rows - 1
    start = jnp.int32(0)
    starts = jnp.zeros((rows, rows), jnp.int32)
    start_last = jnp.int32(0)
    for d in range(docs):
        starts = jnp.where(row >= start, start, starts)
        start_last = jnp.where(last >= start, start, start_last)
        start = start + len_ref[d]
    begin[...] = starts
    for slot in range(n):
        column = rows * (me - slot) + lane
        bias[:, slot * rows:(slot + 1) * rows] = jnp.where(
            (column >= starts) & (column <= row), 0.0, -jnp.inf
        ).astype(F32)
    upper = jnp.where(
        lax.broadcasted_iota(jnp.int32, (rows, rows), 0) <= lane, 1.0, 0.0
    ).astype(F32)
    loads[0].wait()
    logd[...] = dot(-rate_ref[...], upper, ((1,), (0,)), HIGHEST)

    def lanes(head):
        return pl.ds(pl.multiple_of(head * HEAD, HEAD), HEAD)

    def log_rows(head):
        one = logd[pl.ds(head, 1), :]
        return (
            jnp.broadcast_to(one, (rows, rows)),
            jnp.broadcast_to(one[:, rows - 1:], (rows, rows)),
        )

    loads[1].wait()
    loads[2].wait()
    in_tail = first + lane >= start_last

    def inner_pair(pair, _):
        for j in range(PAIR):
            head = pair * PAIR + j
            along, end = log_rows(head)
            weight = jnp.exp(jnp.where(in_tail, end - along, -jnp.inf))
            turned = lk[:, lanes(head)].T * weight
            both = halves(lv[:, lanes(head)])
            lvh[head] = both
            inner[head] = against_columns(halves(turned), both)

        @pl.when(me == 0)
        def _():
            if n > 1:
                state_copy(pair).start()

        return 0

    lax.fori_loop(0, pairs, inner_pair, 0)

    def place_keys(slot):
        at = slice(slot * rows, (slot + 1) * rows)
        cosine, sine = tab[0, at, :], tab[1, at, :]
        for g in range(kv):
            features = slice(g * HEAD, (g + 1) * HEAD)
            high, low = split(rotated(kvbuf[slot, 0, :, features], cosine, sine))
            keys[g, at, :] = jnp.concatenate([high, high], axis=1)
            keys[g, n * rows + slot * rows:n * rows + (slot + 1) * rows, :] = jnp.concatenate(
                [low, low], axis=1
            )
            high, low = split(kvbuf[slot, 1, :, features])
            both = jnp.concatenate([high, low], axis=1)
            vals[g, at, :] = both
            vals[g, n * rows + slot * rows:n * rows + (slot + 1) * rows, :] = both

    def receive(slot):
        @pl.when(me >= slot)
        def _():
            for which in range(2):
                kv_arrival(slot, which).wait_recv()
                if slot < n - 1:
                    @pl.when(me < n - 1)
                    def _():
                        kv_copy(slot, which).start()
            place_keys(slot)

        @pl.when(me < slot)
        def _():
            for g in range(kv):
                for base in (0, n * rows):
                    at = slice(base + slot * rows, base + (slot + 1) * rows)
                    keys[g, at, :] = jnp.zeros((rows, 2 * HEAD), BF16)
                    vals[g, at, :] = jnp.zeros((rows, 2 * HEAD), BF16)

    for copy in loads[3:6]:
        copy.wait()
    if n > 1:
        receive(1)
    place_keys(0)
    for slot in range(2, n):
        receive(slot)
    for copy in loads[6:]:
        copy.wait()

    @pl.when(me == 0)
    def _():
        entered[...] = jnp.zeros_like(entered)

    scale = HEAD ** -0.5

    def finish_pair(pair, _):
        @pl.when((me > 0) & (me < n - 1))
        def _():
            state_copy(pair).wait_recv()
            for j in range(PAIR):
                head = pair * PAIR + j
                _along, end = log_rows(head)
                decay = jnp.exp(jnp.where(start_last < first, end, -jnp.inf))
                inner[head] = inner[head] + decay * entered[head]
            state_copy(pair).start()

        visible = bias[:, 0:rows] == 0.0
        carried = begin[...] < first
        queries = []
        for j in range(PAIR):
            head = pair * PAIR + j
            along, _end = log_rows(head)
            down = along.T
            weight = jnp.exp(jnp.where(visible, down - along, -jnp.inf))
            query = lq[:, lanes(head)]
            scores = against_rows(halves(query), lk[:, lanes(head)]) * weight
            lin[:, lanes(head)] = against_columns(halves(scores), lvh[head])
            reach = jnp.exp(jnp.where(carried, down, -jnp.inf))
            lqh[j] = halves(query * reach)
            turned = rotated(sq[:, lanes(head)], tab[0, 0:rows, :], tab[1, 0:rows, :]) * scale
            queries.append(halves(turned))
        query = jnp.concatenate(queries, axis=0)
        g = lax.div(pair * PAIR, group)
        width = n * rows
        products = dot(query, keys[g], ((1,), (1,)))
        scores = products[:, :width] + products[:, width:]
        scores = scores + jnp.concatenate([bias[...]] * PAIR, axis=0)
        weights = jnp.exp(scores - jnp.max(scores, axis=1, keepdims=True))
        total = jnp.sum(weights, axis=1, keepdims=True)
        mixed = dot(halves(weights), vals[g], ((1,), (0,)))
        mixed = (mixed[:, :HEAD] + mixed[:, HEAD:]) / total
        for j in range(PAIR):
            sm[:, lanes(pair * PAIR + j)] = mixed[j * rows:(j + 1) * rows]
        out_copy(sm, sm_hbm, sm_sem, pair).start()

        if n > 1:
            @pl.when(me == n - 1)
            def _():
                state_copy(pair).wait_recv()

        for j in range(PAIR):
            head = pair * PAIR + j
            attention = lin[:, lanes(head)] + against_columns(lqh[j], halves(entered[head]))
            square = jnp.mean(attention * attention, axis=1, keepdims=True)
            normed = attention * lax.rsqrt(square + EPS) * gain_ref[:, lanes(head)]
            lin[:, lanes(head)] = normed / (1.0 + jnp.exp(-gate[:, lanes(head)]))
        out_copy(lin, lin_hbm, lin_sem, pair).start()
        return 0

    def out_copy(src, dst, sem, pair):
        at = pl.ds(pl.multiple_of(pair * PAIR * HEAD, PAIR * HEAD), PAIR * HEAD)
        return pltpu.make_async_copy(src.at[:, at], dst.at[:, at], sem.at[pair])

    lax.fori_loop(0, pairs, finish_pair, 0)

    def drain(pair, _):
        out_copy(lin, lin_hbm, lin_sem, pair).wait()
        out_copy(sm, sm_hbm, sm_sem, pair).wait()

        @pl.when(me < n - 1)
        def _():
            state_copy(pair).wait_send()

        return 0

    lax.fori_loop(0, pairs, drain, 0)
    for slot in range(n - 1):
        @pl.when((me < n - 1) & (me >= slot))
        def _():
            kv_copy(slot, 0).wait_send()
            kv_copy(slot, 1).wait_send()


def hand_over(rows, lin_in, sm_in, lin_out, sm_out, sem):
    copies = []
    for which, (src, dst) in enumerate([(lin_in, lin_out), (sm_in, sm_out)]):
        for part in range(PARTS):
            at = pl.ds(part * (rows // PARTS), rows // PARTS)
            copies.append(pltpu.make_async_copy(src.at[at], dst.at[at], sem.at[which, part]))
    for copy in copies:
        copy.start()
    for copy in copies:
        copy.wait()


def shards(
    n, lin_query, lin_key, lin_value, lin_gate, decay_rate, norm_gain, sm_query, sm_key, sm_value, doc_lengths
):
    rows, features = lin_query.shape
    heads, kv = features // HEAD, sm_key.shape[1] // HEAD
    docs = doc_lengths.shape[0]
    pairs = heads // PAIR
    width = n * rows
    anywhere = pl.BlockSpec(memory_space=pl.ANY)
    big = pltpu.VMEM((rows, features), F32)
    table = jnp.asarray(rotary_tables(n, rows))
    out = jax.ShapeDtypeStruct((rows, features), F32)
    call = pl.pallas_call(
        functools.partial(kernel, n, rows, heads, kv, docs),
        out_shape=(out, out),
        in_specs=[pl.BlockSpec(memory_space=pltpu.SMEM)] + [anywhere] * 10,
        out_specs=(anywhere, anywhere),
        scratch_shapes=[
            pltpu.VMEM((heads, rows), F32),
            pltpu.VMEM((1, features), F32),
            pltpu.VMEM((n, 2, rows, kv * HEAD), F32),
            big, big, big, big, big,
            pltpu.VMEM((2, width, HEAD), F32),
            big, big,
            pltpu.VMEM((heads, rows), F32),
            pltpu.VMEM((rows, rows), jnp.int32),
            pltpu.VMEM((rows, width), F32),
            pltpu.VMEM((kv, 2 * width, 2 * HEAD), BF16),
            pltpu.VMEM((kv, 2 * width, 2 * HEAD), BF16),
            pltpu.VMEM((heads, rows, 2 * HEAD), BF16),
            pltpu.VMEM((PAIR, rows, 2 * HEAD), BF16),
            pltpu.VMEM((heads, HEAD, HEAD), F32),
            pltpu.VMEM((heads, HEAD, HEAD), F32),
            pltpu.SemaphoreType.DMA((10,)),
            pltpu.SemaphoreType.DMA((n, 2)),
            pltpu.SemaphoreType.DMA((n, 2)),
            pltpu.SemaphoreType.DMA((pairs,)),
            pltpu.SemaphoreType.DMA((pairs,)),
            pltpu.SemaphoreType.DMA((pairs,)),
            pltpu.SemaphoreType.DMA((pairs,)),
        ],
        compiler_params=pltpu.CompilerParams(
            collective_id=0, has_side_effects=True, vmem_limit_bytes=60 * 1024 * 1024
        ),
    )
    results = call(
        doc_lengths, decay_rate, norm_gain.reshape(1, features), sm_key, sm_value,
        lin_key, lin_value, lin_query, sm_query, lin_gate, table,
    )
    return pl.pallas_call(
        functools.partial(hand_over, rows),
        out_shape=(out, out),
        in_specs=[anywhere] * 2,
        out_specs=(anywhere, anywhere),
        scratch_shapes=[pltpu.SemaphoreType.DMA((2, PARTS))],
        compiler_params=pltpu.CompilerParams(vmem_limit_bytes=60 * 1024 * 1024),
    )(*results)


def solution(mesh):
    tokens = P(("dp", "context"), "head")
    in_specs = (
        tokens, tokens, tokens, tokens, P("head", ("dp", "context")), P("head"),
        tokens, tokens, tokens, P("dp"),
    )
    return jax.shard_map(
        functools.partial(shards, mesh.shape["context"]),
        mesh=mesh, in_specs=in_specs, out_specs=(tokens, tokens), check_vma=False,
    )
```

```python
import functools

import jax
import jax.numpy as jnp
import numpy as np
from jax import lax
from jax.experimental import pallas as pl
from jax.experimental.pallas import tpu as pltpu
from jax.sharding import PartitionSpec as P

HEAD = 128
ROT = 64
BASE = 10000000.0
EPS = 1e-05
MESH = pl.DeviceIdType.MESH
HIGHEST = lax.Precision.HIGHEST
F32 = jnp.float32
BF16 = jnp.bfloat16
PAIR = 2
PARTS = 4


def rotary_tables(n, rows):
    half = ROT // 2
    exponent = -(2.0 * np.arange(half, dtype=np.float32)) / np.float32(ROT)
    inverse = np.power(np.float32(BASE), exponent.astype(np.float32)).astype(np.float64)
    place = np.arange(rows)[None, :] - rows * np.arange(n)[:, None]
    angle = place.reshape(-1, 1) * inverse[None, :]
    cosine = np.ones((n * rows, HEAD), np.float32)
    sine = np.zeros((n * rows, HEAD), np.float32)
    cosine[:, :half] = cosine[:, half:ROT] = np.cos(angle)
    sine[:, :half] = -np.sin(angle)
    sine[:, half:ROT] = np.sin(angle)
    return np.stack([cosine, sine])


def dot(a, b, contract, precision=None):
    return lax.dot_general(
        a, b, ((contract[0], contract[1]), ((), ())), precision=precision, preferred_element_type=F32
    )


def split(x):
    high = x.astype(BF16)
    return high, (x - high.astype(F32)).astype(BF16)


def halves(x):
    return jnp.concatenate(split(x), axis=1)


def against_rows(lhs, rhs):
    high, low = split(rhs)
    wide = jnp.concatenate(
        [jnp.concatenate([high, high], axis=1), jnp.concatenate([low, low], axis=1)], axis=0
    )
    out = dot(lhs, wide, ((1,), (1,)))
    return out[:, :HEAD] + out[:, HEAD:]


def against_columns(lhs, rhs):
    out = dot(lhs, jnp.concatenate([rhs, rhs], axis=0), ((1,), (0,)))
    return out[:, :HEAD] + out[:, HEAD:]


def rotated(x, cosine, sine):
    half = ROT // 2
    lane = lax.broadcasted_iota(jnp.int32, x.shape, 1)
    swapped = jnp.where(lane < half, pltpu.roll(x, HEAD - half, 1), pltpu.roll(x, half, 1))
    return x * cosine + swapped * sine


def kernel(
    n, rows, heads, kv, docs,
    len_ref, rate_hbm, gain_hbm, sk_hbm, sv_hbm, lk_hbm, lv_hbm, lq_hbm, sq_hbm, gate_hbm, tab_hbm,
    lin_hbm, sm_hbm,
    rate_ref, gain_ref, kvbuf, lk, lv, lq, sq, gate, tab, lin, sm, logd, begin, bias, keys, vals, lvh, lqh, inner, entered,
    load_sem, kv_send, kv_recv, st_send, st_recv, lin_sem, sm_sem,
):
    me = lax.axis_index("context")
    first = me * rows
    pairs = heads // PAIR
    group = heads // kv
    right = {"context": me + 1}

    barrier = pltpu.get_barrier_semaphore()

    @pl.when(me > 0)
    def _():
        pl.semaphore_signal(barrier, inc=1, device_id={"context": me - 1}, device_id_type=MESH)

    loads = [
        pltpu.make_async_copy(src, dst, load_sem.at[place])
        for place, (src, dst) in enumerate(
            [
                (rate_hbm, rate_ref), (lk_hbm, lk), (lv_hbm, lv), (sk_hbm, kvbuf.at[0, 0]),
                (sv_hbm, kvbuf.at[0, 1]), (tab_hbm, tab), (lq_hbm, lq), (sq_hbm, sq), (gate_hbm, gate),
                (gain_hbm, gain_ref),
            ]
        )
    ]
    for copy in loads[:3]:
        copy.start()

    def kv_copy(slot, which):
        src = (sk_hbm, sv_hbm)[which] if slot == 0 else kvbuf.at[slot, which]
        return pltpu.make_async_remote_copy(
            src_ref=src, dst_ref=kvbuf.at[slot + 1, which],
            send_sem=kv_send.at[slot, which], recv_sem=kv_recv.at[slot + 1, which],
            device_id=right, device_id_type=MESH,
        )

    def kv_arrival(slot, which):
        return pltpu.make_async_remote_copy(
            src_ref=kvbuf.at[slot, which], dst_ref=kvbuf.at[slot, which],
            send_sem=kv_send.at[slot, which], recv_sem=kv_recv.at[slot, which],
            device_id=right, device_id_type=MESH,
        )

    def state_copy(pair):
        here = pl.ds(pair * PAIR, PAIR)
        return pltpu.make_async_remote_copy(
            src_ref=inner.at[here], dst_ref=entered.at[here],
            send_sem=st_send.at[pair], recv_sem=st_recv.at[pair],
            device_id=right, device_id_type=MESH,
        )

    @pl.when(me < n - 1)
    def _():
        pl.semaphore_wait(barrier, 1)
        kv_copy(0, 0).start()
        kv_copy(0, 1).start()

    for copy in loads[3:]:
        copy.start()

    row = first + lax.broadcasted_iota(jnp.int32, (rows, rows), 0)
    lane = lax.broadcasted_iota(jnp.int32, (rows, rows), 1)
    last = first + rows - 1
    start = jnp.int32(0)
    starts = jnp.zeros((rows, rows), jnp.int32)
    start_last = jnp.int32(0)
    for d in range(docs):
        starts = jnp.where(row >= start, start, starts)
        start_last = jnp.where(last >= start, start, start_last)
        start = start + len_ref[d]
    begin[...] = starts
    for slot in range(n):
        column = rows * (me - slot) + lane
        bias[:, slot * rows:(slot + 1) * rows] = jnp.where(
            (column >= starts) & (column <= row), 0.0, -jnp.inf
        ).astype(F32)
    upper = jnp.where(
        lax.broadcasted_iota(jnp.int32, (rows, rows), 0) <= lane, 1.0, 0.0
    ).astype(F32)
    loads[0].wait()
    logd[...] = dot(-rate_ref[...], upper, ((1,), (0,)), HIGHEST)

    def lanes(head):
        return pl.ds(pl.multiple_of(head * HEAD, HEAD), HEAD)

    def log_rows(head):
        one = logd[pl.ds(head, 1), :]
        return (
            jnp.broadcast_to(one, (rows, rows)),
            jnp.broadcast_to(one[:, rows - 1:], (rows, rows)),
        )

    loads[1].wait()
    loads[2].wait()
    in_tail = first + lane >= start_last

    def inner_pair(pair, _):
        for j in range(PAIR):
            head = pair * PAIR + j
            along, end = log_rows(head)
            weight = jnp.exp(jnp.where(in_tail, end - along, -jnp.inf))
            turned = lk[:, lanes(head)].T * weight
            both = halves(lv[:, lanes(head)])
            lvh[head] = both
            inner[head] = against_columns(halves(turned), both)

        @pl.when(me == 0)
        def _():
            if n > 1:
                state_copy(pair).start()

        return 0

    lax.fori_loop(0, pairs, inner_pair, 0)

    def place_keys(slot):
        at = slice(slot * rows, (slot + 1) * rows)
        cosine, sine = tab[0, at, :], tab[1, at, :]
        for g in range(kv):
            features = slice(g * HEAD, (g + 1) * HEAD)
            high, low = split(rotated(kvbuf[slot, 0, :, features], cosine, sine))
            keys[g, at, :] = jnp.concatenate([high, high], axis=1)
            keys[g, n * rows + slot * rows:n * rows + (slot + 1) * rows, :] = jnp.concatenate(
                [low, low], axis=1
            )
            high, low = split(kvbuf[slot, 1, :, features])
            both = jnp.concatenate([high, low], axis=1)
            vals[g, at, :] = both
            vals[g, n * rows + slot * rows:n * rows + (slot + 1) * rows, :] = both

    def receive(slot):
        @pl.when(me >= slot)
        def _():
            for which in range(2):
                kv_arrival(slot, which).wait_recv()
                if slot < n - 1:
                    @pl.when(me < n - 1)
                    def _():
                        kv_copy(slot, which).start()
            place_keys(slot)

        @pl.when(me < slot)
        def _():
            for g in range(kv):
                for base in (0, n * rows):
                    at = slice(base + slot * rows, base + (slot + 1) * rows)
                    keys[g, at, :] = jnp.zeros((rows, 2 * HEAD), BF16)
                    vals[g, at, :] = jnp.zeros((rows, 2 * HEAD), BF16)

    for copy in loads[3:6]:
        copy.wait()
    if n > 1:
        receive(1)
    place_keys(0)
    for slot in range(2, n):
        receive(slot)
    for copy in loads[6:]:
        copy.wait()

    @pl.when(me == 0)
    def _():
        entered[...] = jnp.zeros_like(entered)

    scale = HEAD ** -0.5

    def finish_pair(pair, _):
        @pl.when((me > 0) & (me < n - 1))
        def _():
            state_copy(pair).wait_recv()
            for j in range(PAIR):
                head = pair * PAIR + j
                _along, end = log_rows(head)
                decay = jnp.exp(jnp.where(start_last < first, end, -jnp.inf))
                inner[head] = inner[head] + decay * entered[head]
            state_copy(pair).start()

        visible = bias[:, 0:rows] == 0.0
        carried = begin[...] < first
        queries = []
        for j in range(PAIR):
            head = pair * PAIR + j
            along, _end = log_rows(head)
            down = along.T
            weight = jnp.exp(jnp.where(visible, down - along, -jnp.inf))
            query = lq[:, lanes(head)]
            scores = against_rows(halves(query), lk[:, lanes(head)]) * weight
            lin[:, lanes(head)] = against_columns(halves(scores), lvh[head])
            reach = jnp.exp(jnp.where(carried, down, -jnp.inf))
            lqh[j] = halves(query * reach)
            turned = rotated(sq[:, lanes(head)], tab[0, 0:rows, :], tab[1, 0:rows, :]) * scale
            queries.append(halves(turned))
        query = jnp.concatenate(queries, axis=0)
        g = lax.div(pair * PAIR, group)
        width = n * rows
        products = dot(query, keys[g], ((1,), (1,)))
        scores = products[:, :width] + products[:, width:]
        scores = scores + jnp.concatenate([bias[...]] * PAIR, axis=0)
        weights = jnp.exp(scores - jnp.max(scores, axis=1, keepdims=True))
        total = jnp.sum(weights, axis=1, keepdims=True)
        mixed = dot(halves(weights), vals[g], ((1,), (0,)))
        mixed = (mixed[:, :HEAD] + mixed[:, HEAD:]) / total
        for j in range(PAIR):
            sm[:, lanes(pair * PAIR + j)] = mixed[j * rows:(j + 1) * rows]
        out_copy(sm, sm_hbm, sm_sem, pair).start()

        if n > 1:
            @pl.when(me == n - 1)
            def _():
                state_copy(pair).wait_recv()

        for j in range(PAIR):
            head = pair * PAIR + j
            attention = lin[:, lanes(head)] + against_columns(lqh[j], halves(entered[head]))
            square = jnp.mean(attention * attention, axis=1, keepdims=True)
            normed = attention * lax.rsqrt(square + EPS) * gain_ref[:, lanes(head)]
            lin[:, lanes(head)] = normed / (1.0 + jnp.exp(-gate[:, lanes(head)]))
        out_copy(lin, lin_hbm, lin_sem, pair).start()
        return 0

    def out_copy(src, dst, sem, pair):
        at = pl.ds(pl.multiple_of(pair * PAIR * HEAD, PAIR * HEAD), PAIR * HEAD)
        return pltpu.make_async_copy(src.at[:, at], dst.at[:, at], sem.at[pair])

    lax.fori_loop(0, pairs, finish_pair, 0)

    def drain(pair, _):
        out_copy(lin, lin_hbm, lin_sem, pair).wait()
        out_copy(sm, sm_hbm, sm_sem, pair).wait()

        @pl.when(me < n - 1)
        def _():
            state_copy(pair).wait_send()

        return 0

    lax.fori_loop(0, pairs, drain, 0)
    for slot in range(n - 1):
        @pl.when((me < n - 1) & (me >= slot))
        def _():
            kv_copy(slot, 0).wait_send()
            kv_copy(slot, 1).wait_send()


def hand_over(rows, lin_in, sm_in, lin_out, sm_out, held, in_sem, out_sem):
    arrive, leave = [], []
    for part in range(PARTS):
        at = pl.ds(part * (rows // PARTS), rows // PARTS)
        for which, (src, dst) in enumerate([(lin_in, lin_out), (sm_in, sm_out)]):
            slot = held.at[which, at]
            arrive.append(pltpu.make_async_copy(src.at[at], slot, in_sem.at[which, part]))
            leave.append(pltpu.make_async_copy(slot, dst.at[at], out_sem.at[which, part]))
    for copy in arrive:
        copy.start()
    for come, go in zip(arrive, leave):
        come.wait()
        go.start()
    for copy in leave:
        copy.wait()


def shards(
    n, lin_query, lin_key, lin_value, lin_gate, decay_rate, norm_gain, sm_query, sm_key, sm_value, doc_lengths
):
    rows, features = lin_query.shape
    heads, kv = features // HEAD, sm_key.shape[1] // HEAD
    docs = doc_lengths.shape[0]
    pairs = heads // PAIR
    width = n * rows
    anywhere = pl.BlockSpec(memory_space=pl.ANY)
    big = pltpu.VMEM((rows, features), F32)
    table = jnp.asarray(rotary_tables(n, rows))
    out = jax.ShapeDtypeStruct((rows, features), F32)
    call = pl.pallas_call(
        functools.partial(kernel, n, rows, heads, kv, docs),
        out_shape=(out, out),
        in_specs=[pl.BlockSpec(memory_space=pltpu.SMEM)] + [anywhere] * 10,
        out_specs=(anywhere, anywhere),
        scratch_shapes=[
            pltpu.VMEM((heads, rows), F32),
            pltpu.VMEM((1, features), F32),
            pltpu.VMEM((n, 2, rows, kv * HEAD), F32),
            big, big, big, big, big,
            pltpu.VMEM((2, width, HEAD), F32),
            big, big,
            pltpu.VMEM((heads, rows), F32),
            pltpu.VMEM((rows, rows), jnp.int32),
            pltpu.VMEM((rows, width), F32),
            pltpu.VMEM((kv, 2 * width, 2 * HEAD), BF16),
            pltpu.VMEM((kv, 2 * width, 2 * HEAD), BF16),
            pltpu.VMEM((heads, rows, 2 * HEAD), BF16),
            pltpu.VMEM((PAIR, rows, 2 * HEAD), BF16),
            pltpu.VMEM((heads, HEAD, HEAD), F32),
            pltpu.VMEM((heads, HEAD, HEAD), F32),
            pltpu.SemaphoreType.DMA((10,)),
            pltpu.SemaphoreType.DMA((n, 2)),
            pltpu.SemaphoreType.DMA((n, 2)),
            pltpu.SemaphoreType.DMA((pairs,)),
            pltpu.SemaphoreType.DMA((pairs,)),
            pltpu.SemaphoreType.DMA((pairs,)),
            pltpu.SemaphoreType.DMA((pairs,)),
        ],
        compiler_params=pltpu.CompilerParams(
            collective_id=0, has_side_effects=True, vmem_limit_bytes=60 * 1024 * 1024
        ),
    )
    results = call(
        doc_lengths, decay_rate, norm_gain.reshape(1, features), sm_key, sm_value,
        lin_key, lin_value, lin_query, sm_query, lin_gate, table,
    )
    return pl.pallas_call(
        functools.partial(hand_over, rows),
        out_shape=(out, out),
        in_specs=[anywhere] * 2,
        out_specs=(anywhere, anywhere),
        scratch_shapes=[
            pltpu.VMEM((2, rows, features), F32),
            pltpu.SemaphoreType.DMA((2, PARTS)),
            pltpu.SemaphoreType.DMA((2, PARTS)),
        ],
        compiler_params=pltpu.CompilerParams(vmem_limit_bytes=60 * 1024 * 1024),
    )(*results)


def solution(mesh):
    tokens = P(("dp", "context"), "head")
    in_specs = (
        tokens, tokens, tokens, tokens, P("head", ("dp", "context")), P("head"),
        tokens, tokens, tokens, P("dp"),
    )
    return jax.shard_map(
        functools.partial(shards, mesh.shape["context"]),
        mesh=mesh, in_specs=in_specs, out_specs=(tokens, tokens), check_vma=False,
    )
```

```python
import functools

import jax
import jax.numpy as jnp
import numpy as np
from jax import lax
from jax.experimental import pallas as pl
from jax.experimental.pallas import tpu as pltpu
from jax.sharding import PartitionSpec as P

HEAD = 128
ROT = 64
BASE = 10000000.0
EPS = 1e-05
MESH = pl.DeviceIdType.MESH
HIGHEST = lax.Precision.HIGHEST
F32 = jnp.float32
BF16 = jnp.bfloat16
PAIR = 2
PARTS = 4


def rotary_tables(n, rows):
    half = ROT // 2
    exponent = -(2.0 * np.arange(half, dtype=np.float32)) / np.float32(ROT)
    inverse = np.power(np.float32(BASE), exponent.astype(np.float32)).astype(np.float64)
    place = np.arange(rows)[None, :] - rows * np.arange(n)[:, None]
    angle = place.reshape(-1, 1) * inverse[None, :]
    cosine = np.ones((n * rows, HEAD), np.float32)
    sine = np.zeros((n * rows, HEAD), np.float32)
    cosine[:, :half] = cosine[:, half:ROT] = np.cos(angle)
    sine[:, :half] = -np.sin(angle)
    sine[:, half:ROT] = np.sin(angle)
    return np.stack([cosine, sine])


def dot(a, b, contract, precision=None):
    return lax.dot_general(
        a, b, ((contract[0], contract[1]), ((), ())), precision=precision, preferred_element_type=F32
    )


def split(x):
    high = x.astype(BF16)
    return high, (x - high.astype(F32)).astype(BF16)


def halves(x):
    return jnp.concatenate(split(x), axis=1)


def against_rows(lhs, rhs):
    high, low = split(rhs)
    wide = jnp.concatenate(
        [jnp.concatenate([high, high], axis=1), jnp.concatenate([low, low], axis=1)], axis=0
    )
    out = dot(lhs, wide, ((1,), (1,)))
    return out[:, :HEAD] + out[:, HEAD:]


def against_columns(lhs, rhs):
    out = dot(lhs, jnp.concatenate([rhs, rhs], axis=0), ((1,), (0,)))
    return out[:, :HEAD] + out[:, HEAD:]


def rotated(x, cosine, sine):
    half = ROT // 2
    lane = lax.broadcasted_iota(jnp.int32, x.shape, 1)
    swapped = jnp.where(lane < half, pltpu.roll(x, HEAD - half, 1), pltpu.roll(x, half, 1))
    return x * cosine + swapped * sine


def kernel(
    n, rows, heads, kv, docs,
    len_ref, rate_hbm, gain_hbm, sk_hbm, sv_hbm, lk_hbm, lv_hbm, lq_hbm, sq_hbm, gate_hbm, tab_hbm,
    lin_hbm, sm_hbm,
    rate_ref, gain_ref, kvbuf, lk, lv, lq, sq, gate, tab, lin, sm, logd, begin, bias, keys, vals, lvh, lqh, reached, asked, inner, entered,
    load_sem, kv_send, kv_recv, st_send, st_recv, lin_sem, sm_sem, ask_send, ask_recv,
):
    me = lax.axis_index("context")
    first = me * rows
    pairs = heads // PAIR
    group = heads // kv
    right = {"context": me + 1}
    pack = n > 1 and 4 * (n - 1) == 3 * n
    packed_pairs = -(-2 * kv // PAIR) if pack else 0

    barrier = pltpu.get_barrier_semaphore()

    @pl.when(me > 0)
    def _():
        pl.semaphore_signal(barrier, inc=1, device_id={"context": me - 1}, device_id_type=MESH)

    if pack:
        @pl.when(me == n - 2)
        def _():
            pl.semaphore_signal(barrier, inc=1, device_id=right, device_id_type=MESH)

    loads = [
        pltpu.make_async_copy(src, dst, load_sem.at[place])
        for place, (src, dst) in enumerate(
            [
                (rate_hbm, rate_ref), (lk_hbm, lk), (lv_hbm, lv), (sk_hbm, kvbuf.at[0, 0]),
                (sv_hbm, kvbuf.at[0, 1]), (tab_hbm, tab), (lq_hbm, lq), (sq_hbm, sq), (gate_hbm, gate),
                (gain_hbm, gain_ref),
            ]
        )
    ]
    for copy in loads[:3]:
        copy.start()

    def kv_copy(slot, which):
        src = (sk_hbm, sv_hbm)[which] if slot == 0 else kvbuf.at[slot, which]
        return pltpu.make_async_remote_copy(
            src_ref=src, dst_ref=kvbuf.at[slot + 1, which],
            send_sem=kv_send.at[slot, which], recv_sem=kv_recv.at[slot + 1, which],
            device_id=right, device_id_type=MESH,
        )

    def kv_arrival(slot, which):
        return pltpu.make_async_remote_copy(
            src_ref=kvbuf.at[slot, which], dst_ref=kvbuf.at[slot, which],
            send_sem=kv_send.at[slot, which], recv_sem=kv_recv.at[slot, which],
            device_id=right, device_id_type=MESH,
        )

    def state_copy(pair):
        here = pl.ds(pair * PAIR, PAIR)
        return pltpu.make_async_remote_copy(
            src_ref=inner.at[here], dst_ref=entered.at[here],
            send_sem=st_send.at[pair], recv_sem=st_recv.at[pair],
            device_id=right, device_id_type=MESH,
        )

    def query_copy(pair):
        at = pl.ds(pl.multiple_of(pair * PAIR * HEAD, PAIR * HEAD), PAIR * HEAD)
        return pltpu.make_async_remote_copy(
            src_ref=lq_hbm.at[:, at], dst_ref=asked.at[:, at],
            send_sem=ask_send.at[pair], recv_sem=ask_recv.at[pair],
            device_id={"context": me - 1}, device_id_type=MESH,
        )

    @pl.when(me < n - 1)
    def _():
        pl.semaphore_wait(barrier, 1)
        kv_copy(0, 0).start()
        kv_copy(0, 1).start()

    if pack:
        @pl.when(me == n - 1)
        def _():
            pl.semaphore_wait(barrier, 1)
            for pair in range(pairs):
                query_copy(pair).start()

    for copy in loads[3:]:
        copy.start()

    row = first + lax.broadcasted_iota(jnp.int32, (rows, rows), 0)
    lane = lax.broadcasted_iota(jnp.int32, (rows, rows), 1)
    last = first + rows - 1
    start = jnp.int32(0)
    starts = jnp.zeros((rows, rows), jnp.int32)
    start_last = start_next = jnp.int32(0)
    for d in range(docs):
        starts = jnp.where(row >= start, start, starts)
        start_last = jnp.where(last >= start, start, start_last)
        start_next = jnp.where(last + 1 >= start, start, start_next)
        start = start + len_ref[d]
    begin[...] = starts
    for slot in range(n):
        column = rows * (me - slot) + lane
        bias[:, slot * rows:(slot + 1) * rows] = jnp.where(
            (column >= starts) & (column <= row), 0.0, -jnp.inf
        ).astype(F32)
    upper = jnp.where(
        lax.broadcasted_iota(jnp.int32, (rows, rows), 0) <= lane, 1.0, 0.0
    ).astype(F32)
    loads[0].wait()
    logd[...] = dot(-rate_ref[...], upper, ((1,), (0,)), HIGHEST)

    def lanes(head):
        return pl.ds(pl.multiple_of(head * HEAD, HEAD), HEAD)

    def log_rows(head):
        one = logd[pl.ds(head, 1), :]
        return (
            jnp.broadcast_to(one, (rows, rows)),
            jnp.broadcast_to(one[:, rows - 1:], (rows, rows)),
        )

    loads[1].wait()
    loads[2].wait()
    in_tail = first + lane >= start_last

    def inner_pair(pair, _):
        for j in range(PAIR):
            head = pair * PAIR + j
            along, end = log_rows(head)
            weight = jnp.exp(jnp.where(in_tail, end - along, -jnp.inf))
            turned = lk[:, lanes(head)].T * weight
            both = halves(lv[:, lanes(head)])
            lvh[head] = both
            inner[head] = against_columns(halves(turned), both)

        @pl.when(me == 0)
        def _():
            if n > 1:
                state_copy(pair).start()

        return 0

    lax.fori_loop(0, pairs, inner_pair, 0)

    def place_keys(slot, source):
        at = slice(slot * rows, (slot + 1) * rows)
        cosine, sine = tab[0, at, :], tab[1, at, :]
        for g in range(kv):
            high, low = split(rotated(source(0, g), cosine, sine))
            keys[g, at, :] = jnp.concatenate([high, high], axis=1)
            keys[g, n * rows + slot * rows:n * rows + (slot + 1) * rows, :] = jnp.concatenate(
                [low, low], axis=1
            )
            high, low = split(source(1, g))
            both = jnp.concatenate([high, low], axis=1)
            vals[g, at, :] = both
            vals[g, n * rows + slot * rows:n * rows + (slot + 1) * rows, :] = both

    def from_slot(slot):
        return lambda which, g: kvbuf[slot, which, :, g * HEAD:(g + 1) * HEAD]

    def receive(slot):
        @pl.when(me >= slot)
        def _():
            if pack and slot == n - 1:
                for pair in range(packed_pairs):
                    state_copy(pair).wait_recv()
                place_keys(slot, lambda which, g: entered[which * kv + g])
                return
            for which in range(2):
                kv_arrival(slot, which).wait_recv()
                if slot < n - 1 - pack:
                    @pl.when(me < n - 1)
                    def _():
                        kv_copy(slot, which).start()
            place_keys(slot, from_slot(slot))

        @pl.when(me < slot)
        def _():
            for g in range(kv):
                for base in (0, n * rows):
                    at = slice(base + slot * rows, base + (slot + 1) * rows)
                    keys[g, at, :] = jnp.zeros((rows, 2 * HEAD), BF16)
                    vals[g, at, :] = jnp.zeros((rows, 2 * HEAD), BF16)

    for copy in loads[3:6]:
        copy.wait()
    if n > 1:
        receive(1)
    place_keys(0, from_slot(0))
    for slot in range(2, n):
        receive(slot)
    for copy in loads[6:]:
        copy.wait()

    @pl.when(me == 0)
    def _():
        entered[...] = jnp.zeros_like(entered)

    scale = HEAD ** -0.5

    def answer(pair):
        query_copy(pair).wait_recv()
        kept = row - (n - 2) * rows >= start_next
        for j in range(PAIR):
            head = pair * PAIR + j
            inner[head] = against_columns(halves(asked[:, lanes(head)]), halves(inner[head]))

            @pl.when(head < 2 * kv)
            def _():
                piece = kvbuf[n - 2, lax.div(head, kv), :, lanes(lax.rem(head, kv))]
                inner[head] = jnp.where(kept, piece, inner[head])

    def finish_pair(pair, _):
        @pl.when((me > 0) & (me < n - 1))
        def _():
            state_copy(pair).wait_recv()
            for j in range(PAIR):
                head = pair * PAIR + j
                _along, end = log_rows(head)
                decay = jnp.exp(jnp.where(start_last < first, end, -jnp.inf))
                inner[head] = inner[head] + decay * entered[head]
            if pack:
                @pl.when(me == n - 2)
                def _():
                    answer(pair)
            state_copy(pair).start()

        visible = bias[:, 0:rows] == 0.0
        carried = begin[...] < first
        queries = []
        for j in range(PAIR):
            head = pair * PAIR + j
            along, _end = log_rows(head)
            down = along.T
            weight = jnp.exp(jnp.where(visible, down - along, -jnp.inf))
            query = lq[:, lanes(head)]
            scores = against_rows(halves(query), lk[:, lanes(head)]) * weight
            lin[:, lanes(head)] = against_columns(halves(scores), lvh[head])
            reach = jnp.exp(jnp.where(carried, down, -jnp.inf))
            lqh[j] = halves(query * reach)
            reached[j] = reach
            turned = rotated(sq[:, lanes(head)], tab[0, 0:rows, :], tab[1, 0:rows, :]) * scale
            queries.append(halves(turned))
        query = jnp.concatenate(queries, axis=0)
        g = lax.div(pair * PAIR, group)
        width = n * rows
        products = dot(query, keys[g], ((1,), (1,)))
        scores = products[:, :width] + products[:, width:]
        scores = scores + jnp.concatenate([bias[...]] * PAIR, axis=0)
        weights = jnp.exp(scores - jnp.max(scores, axis=1, keepdims=True))
        total = jnp.sum(weights, axis=1, keepdims=True)
        mixed = dot(halves(weights), vals[g], ((1,), (0,)))
        mixed = (mixed[:, :HEAD] + mixed[:, HEAD:]) / total
        for j in range(PAIR):
            sm[:, lanes(pair * PAIR + j)] = mixed[j * rows:(j + 1) * rows]
        out_copy(sm, sm_hbm, sm_sem, pair).start()

        if n > 1:
            @pl.when((me == n - 1) & (pair >= packed_pairs))
            def _():
                state_copy(pair).wait_recv()

        for j in range(PAIR):
            head = pair * PAIR + j
            if pack:
                @pl.when(me == n - 1)
                def _():
                    lin[:, lanes(head)] += reached[j] * entered[head]

                @pl.when(me < n - 1)
                def _():
                    lin[:, lanes(head)] += against_columns(lqh[j], halves(entered[head]))

                attention = lin[:, lanes(head)]
            else:
                attention = lin[:, lanes(head)] + against_columns(lqh[j], halves(entered[head]))
            square = jnp.mean(attention * attention, axis=1, keepdims=True)
            normed = attention * lax.rsqrt(square + EPS) * gain_ref[:, lanes(head)]
            lin[:, lanes(head)] = normed / (1.0 + jnp.exp(-gate[:, lanes(head)]))
        out_copy(lin, lin_hbm, lin_sem, pair).start()
        return 0

    def out_copy(src, dst, sem, pair):
        at = pl.ds(pl.multiple_of(pair * PAIR * HEAD, PAIR * HEAD), PAIR * HEAD)
        return pltpu.make_async_copy(src.at[:, at], dst.at[:, at], sem.at[pair])

    lax.fori_loop(0, pairs, finish_pair, 0)

    def drain(pair, _):
        out_copy(lin, lin_hbm, lin_sem, pair).wait()
        out_copy(sm, sm_hbm, sm_sem, pair).wait()

        @pl.when(me < n - 1)
        def _():
            state_copy(pair).wait_send()

        if pack:
            @pl.when(me == n - 1)
            def _():
                query_copy(pair).wait_send()

        return 0

    lax.fori_loop(0, pairs, drain, 0)
    for slot in range(n - 1 - pack):
        @pl.when((me < n - 1) & (me >= slot))
        def _():
            kv_copy(slot, 0).wait_send()
            kv_copy(slot, 1).wait_send()


def hand_over(rows, lin_in, sm_in, lin_out, sm_out, held, in_sem, out_sem):
    arrive, leave = [], []
    for part in range(PARTS):
        at = pl.ds(part * (rows // PARTS), rows // PARTS)
        for which, (src, dst) in enumerate([(lin_in, lin_out), (sm_in, sm_out)]):
            slot = held.at[which, at]
            arrive.append(pltpu.make_async_copy(src.at[at], slot, in_sem.at[which, part]))
            leave.append(pltpu.make_async_copy(slot, dst.at[at], out_sem.at[which, part]))
    for copy in arrive:
        copy.start()
    for come, go in zip(arrive, leave):
        come.wait()
        go.start()
    for copy in leave:
        copy.wait()


def shards(
    n, lin_query, lin_key, lin_value, lin_gate, decay_rate, norm_gain, sm_query, sm_key, sm_value, doc_lengths
):
    rows, features = lin_query.shape
    heads, kv = features // HEAD, sm_key.shape[1] // HEAD
    docs = doc_lengths.shape[0]
    pairs = heads // PAIR
    width = n * rows
    anywhere = pl.BlockSpec(memory_space=pl.ANY)
    big = pltpu.VMEM((rows, features), F32)
    table = jnp.asarray(rotary_tables(n, rows))
    out = jax.ShapeDtypeStruct((rows, features), F32)
    call = pl.pallas_call(
        functools.partial(kernel, n, rows, heads, kv, docs),
        out_shape=(out, out),
        in_specs=[pl.BlockSpec(memory_space=pltpu.SMEM)] + [anywhere] * 10,
        out_specs=(anywhere, anywhere),
        scratch_shapes=[
            pltpu.VMEM((heads, rows), F32),
            pltpu.VMEM((1, features), F32),
            pltpu.VMEM((n, 2, rows, kv * HEAD), F32),
            big, big, big, big, big,
            pltpu.VMEM((2, width, HEAD), F32),
            big, big,
            pltpu.VMEM((heads, rows), F32),
            pltpu.VMEM((rows, rows), jnp.int32),
            pltpu.VMEM((rows, width), F32),
            pltpu.VMEM((kv, 2 * width, 2 * HEAD), BF16),
            pltpu.VMEM((kv, 2 * width, 2 * HEAD), BF16),
            pltpu.VMEM((heads, rows, 2 * HEAD), BF16),
            pltpu.VMEM((PAIR, rows, 2 * HEAD), BF16),
            pltpu.VMEM((PAIR, rows, rows), F32),
            big,
            pltpu.VMEM((heads, HEAD, HEAD), F32),
            pltpu.VMEM((heads, HEAD, HEAD), F32),
            pltpu.SemaphoreType.DMA((10,)),
            pltpu.SemaphoreType.DMA((n, 2)),
            pltpu.SemaphoreType.DMA((n, 2)),
            pltpu.SemaphoreType.DMA((pairs,)),
            pltpu.SemaphoreType.DMA((pairs,)),
            pltpu.SemaphoreType.DMA((pairs,)),
            pltpu.SemaphoreType.DMA((pairs,)),
            pltpu.SemaphoreType.DMA((pairs,)),
            pltpu.SemaphoreType.DMA((pairs,)),
        ],
        compiler_params=pltpu.CompilerParams(
            collective_id=0, has_side_effects=True, vmem_limit_bytes=60 * 1024 * 1024
        ),
    )
    results = call(
        doc_lengths, decay_rate, norm_gain.reshape(1, features), sm_key, sm_value,
        lin_key, lin_value, lin_query, sm_query, lin_gate, table,
    )
    return pl.pallas_call(
        functools.partial(hand_over, rows),
        out_shape=(out, out),
        in_specs=[anywhere] * 2,
        out_specs=(anywhere, anywhere),
        scratch_shapes=[
            pltpu.VMEM((2, rows, features), F32),
            pltpu.SemaphoreType.DMA((2, PARTS)),
            pltpu.SemaphoreType.DMA((2, PARTS)),
        ],
        compiler_params=pltpu.CompilerParams(vmem_limit_bytes=60 * 1024 * 1024),
    )(*results)


def solution(mesh):
    tokens = P(("dp", "context"), "head")
    in_specs = (
        tokens, tokens, tokens, tokens, P("head", ("dp", "context")), P("head"),
        tokens, tokens, tokens, P("dp"),
    )
    return jax.shard_map(
        functools.partial(shards, mesh.shape["context"]),
        mesh=mesh, in_specs=in_specs, out_specs=(tokens, tokens), check_vma=False,
    )
```

```python
import functools

import jax
import jax.numpy as jnp
import numpy as np
from jax import lax
from jax.experimental import pallas as pl
from jax.experimental.pallas import tpu as pltpu
from jax.sharding import PartitionSpec as P

HEAD = 128
ROT = 64
BASE = 10000000.0
EPS = 1e-05
MESH = pl.DeviceIdType.MESH
HIGHEST = lax.Precision.HIGHEST
F32 = jnp.float32
BF16 = jnp.bfloat16
PAIR = 2
PARTS = 4


def rotary_tables(n, rows):
    half = ROT // 2
    exponent = -(2.0 * np.arange(half, dtype=np.float32)) / np.float32(ROT)
    inverse = np.power(np.float32(BASE), exponent.astype(np.float32)).astype(np.float64)
    place = np.arange(rows)[None, :] - rows * np.arange(n)[:, None]
    angle = place.reshape(-1, 1) * inverse[None, :]
    cosine = np.ones((n * rows, HEAD), np.float32)
    sine = np.zeros((n * rows, HEAD), np.float32)
    cosine[:, :half] = cosine[:, half:ROT] = np.cos(angle)
    sine[:, :half] = -np.sin(angle)
    sine[:, half:ROT] = np.sin(angle)
    return np.stack([cosine, sine])


def dot(a, b, contract, precision=None):
    return lax.dot_general(
        a, b, ((contract[0], contract[1]), ((), ())), precision=precision, preferred_element_type=F32
    )


def split(x):
    high = x.astype(BF16)
    return high, (x - high.astype(F32)).astype(BF16)


def halves(x):
    return jnp.concatenate(split(x), axis=1)


def against_rows(lhs, rhs):
    high, low = split(rhs)
    wide = jnp.concatenate(
        [jnp.concatenate([high, high], axis=1), jnp.concatenate([low, low], axis=1)], axis=0
    )
    out = dot(lhs, wide, ((1,), (1,)))
    return out[:, :HEAD] + out[:, HEAD:]


def against_columns(lhs, rhs):
    out = dot(lhs, jnp.concatenate([rhs, rhs], axis=0), ((1,), (0,)))
    return out[:, :HEAD] + out[:, HEAD:]


def rotated(x, cosine, sine):
    half = ROT // 2
    lane = lax.broadcasted_iota(jnp.int32, x.shape, 1)
    swapped = jnp.where(lane < half, pltpu.roll(x, HEAD - half, 1), pltpu.roll(x, half, 1))
    return x * cosine + swapped * sine


def kernel(
    n, rows, heads, kv, docs,
    len_ref, rate_hbm, gain_hbm, sk_hbm, sv_hbm, lk_hbm, lv_hbm, lq_hbm, sq_hbm, gate_hbm, tab_hbm,
    lin_hbm, sm_hbm,
    rate_ref, gain_ref, kvbuf, lk, lv, lq, sq, gate, tab, lin, sm, logd, begin, bias, keys, vals, lvh, lqh, reached, asked, inner, entered,
    load_sem, kv_send, kv_recv, st_send, st_recv, lin_sem, sm_sem, ask_send, ask_recv,
):
    me = lax.axis_index("context")
    first = me * rows
    pairs = heads // PAIR
    group = heads // kv
    right = {"context": me + 1}
    pack = n > 1 and 4 * (n - 1) == 3 * n
    packed_pairs = -(-2 * kv // PAIR) if pack else 0

    barrier = pltpu.get_barrier_semaphore()

    @pl.when(me > 0)
    def _():
        pl.semaphore_signal(barrier, inc=1, device_id={"context": me - 1}, device_id_type=MESH)

    if pack:
        @pl.when(me == n - 2)
        def _():
            pl.semaphore_signal(barrier, inc=1, device_id=right, device_id_type=MESH)

    loads = [
        pltpu.make_async_copy(src, dst, load_sem.at[place])
        for place, (src, dst) in enumerate(
            [
                (rate_hbm, rate_ref), (lk_hbm, lk), (lv_hbm, lv), (sk_hbm, kvbuf.at[0, 0]),
                (sv_hbm, kvbuf.at[0, 1]), (tab_hbm, tab), (lq_hbm, lq), (sq_hbm, sq), (gate_hbm, gate),
                (gain_hbm, gain_ref),
            ]
        )
    ]
    for copy in loads[:3]:
        copy.start()

    def kv_copy(slot, which):
        src = (sk_hbm, sv_hbm)[which] if slot == 0 else kvbuf.at[slot, which]
        return pltpu.make_async_remote_copy(
            src_ref=src, dst_ref=kvbuf.at[slot + 1, which],
            send_sem=kv_send.at[slot, which], recv_sem=kv_recv.at[slot + 1, which],
            device_id=right, device_id_type=MESH,
        )

    def kv_arrival(slot, which):
        return pltpu.make_async_remote_copy(
            src_ref=kvbuf.at[slot, which], dst_ref=kvbuf.at[slot, which],
            send_sem=kv_send.at[slot, which], recv_sem=kv_recv.at[slot, which],
            device_id=right, device_id_type=MESH,
        )

    def state_copy(head):
        return pltpu.make_async_remote_copy(
            src_ref=inner.at[head], dst_ref=entered.at[head],
            send_sem=st_send.at[head], recv_sem=st_recv.at[head],
            device_id=right, device_id_type=MESH,
        )

    def query_copy(pair):
        at = pl.ds(pl.multiple_of(pair * PAIR * HEAD, PAIR * HEAD), PAIR * HEAD)
        return pltpu.make_async_remote_copy(
            src_ref=lq_hbm.at[:, at], dst_ref=asked.at[:, at],
            send_sem=ask_send.at[pair], recv_sem=ask_recv.at[pair],
            device_id={"context": me - 1}, device_id_type=MESH,
        )

    @pl.when(me < n - 1)
    def _():
        pl.semaphore_wait(barrier, 1)
        kv_copy(0, 0).start()
        kv_copy(0, 1).start()

    if pack:
        @pl.when(me == n - 1)
        def _():
            pl.semaphore_wait(barrier, 1)
            for pair in range(pairs):
                query_copy(pair).start()

    for copy in loads[3:]:
        copy.start()

    row = first + lax.broadcasted_iota(jnp.int32, (rows, rows), 0)
    lane = lax.broadcasted_iota(jnp.int32, (rows, rows), 1)
    last = first + rows - 1
    start = jnp.int32(0)
    starts = jnp.zeros((rows, rows), jnp.int32)
    start_last = start_next = jnp.int32(0)
    for d in range(docs):
        starts = jnp.where(row >= start, start, starts)
        start_last = jnp.where(last >= start, start, start_last)
        start_next = jnp.where(last + 1 >= start, start, start_next)
        start = start + len_ref[d]
    begin[...] = starts
    for slot in range(n):
        column = rows * (me - slot) + lane
        bias[:, slot * rows:(slot + 1) * rows] = jnp.where(
            (column >= starts) & (column <= row), 0.0, -jnp.inf
        ).astype(F32)
    upper = jnp.where(
        lax.broadcasted_iota(jnp.int32, (rows, rows), 0) <= lane, 1.0, 0.0
    ).astype(F32)
    loads[0].wait()
    logd[...] = dot(-rate_ref[...], upper, ((1,), (0,)), HIGHEST)

    def lanes(head):
        return pl.ds(pl.multiple_of(head * HEAD, HEAD), HEAD)

    def log_rows(head):
        one = logd[pl.ds(head, 1), :]
        return (
            jnp.broadcast_to(one, (rows, rows)),
            jnp.broadcast_to(one[:, rows - 1:], (rows, rows)),
        )

    loads[1].wait()
    loads[2].wait()
    in_tail = first + lane >= start_last

    def inner_pair(pair, _):
        for j in range(PAIR):
            head = pair * PAIR + j
            along, end = log_rows(head)
            weight = jnp.exp(jnp.where(in_tail, end - along, -jnp.inf))
            turned = lk[:, lanes(head)].T * weight
            both = halves(lv[:, lanes(head)])
            lvh[head] = both
            inner[head] = against_columns(halves(turned), both)

        @pl.when(me == 0)
        def _():
            if n > 1:
                for j in range(PAIR):
                    state_copy(pair * PAIR + j).start()

        return 0

    lax.fori_loop(0, pairs, inner_pair, 0)

    def place_keys(slot, source):
        at = slice(slot * rows, (slot + 1) * rows)
        cosine, sine = tab[0, at, :], tab[1, at, :]
        for g in range(kv):
            high, low = split(rotated(source(0, g), cosine, sine))
            keys[g, at, :] = jnp.concatenate([high, high], axis=1)
            keys[g, n * rows + slot * rows:n * rows + (slot + 1) * rows, :] = jnp.concatenate(
                [low, low], axis=1
            )
            high, low = split(source(1, g))
            both = jnp.concatenate([high, low], axis=1)
            vals[g, at, :] = both
            vals[g, n * rows + slot * rows:n * rows + (slot + 1) * rows, :] = both

    def from_slot(slot):
        return lambda which, g: kvbuf[slot, which, :, g * HEAD:(g + 1) * HEAD]

    def receive(slot):
        @pl.when(me >= slot)
        def _():
            if pack and slot == n - 1:
                for head in range(packed_pairs * PAIR):
                    state_copy(head).wait_recv()
                place_keys(slot, lambda which, g: entered[which * kv + g])
                return
            for which in range(2):
                kv_arrival(slot, which).wait_recv()
                if slot < n - 1 - pack:
                    @pl.when(me < n - 1)
                    def _():
                        kv_copy(slot, which).start()
            place_keys(slot, from_slot(slot))

        @pl.when(me < slot)
        def _():
            for g in range(kv):
                for base in (0, n * rows):
                    at = slice(base + slot * rows, base + (slot + 1) * rows)
                    keys[g, at, :] = jnp.zeros((rows, 2 * HEAD), BF16)
                    vals[g, at, :] = jnp.zeros((rows, 2 * HEAD), BF16)

    for copy in loads[3:6]:
        copy.wait()
    if n > 1:
        receive(1)
    place_keys(0, from_slot(0))
    for slot in range(2, n):
        receive(slot)
    for copy in loads[6:]:
        copy.wait()

    @pl.when(me == 0)
    def _():
        entered[...] = jnp.zeros_like(entered)

    scale = HEAD ** -0.5

    def answer(pair, j):
        if j == 0:
            query_copy(pair).wait_recv()
        kept = row - (n - 2) * rows >= start_next
        head = pair * PAIR + j
        inner[head] = against_columns(halves(asked[:, lanes(head)]), halves(inner[head]))

        @pl.when(head < 2 * kv)
        def _():
            piece = kvbuf[n - 2, lax.div(head, kv), :, lanes(lax.rem(head, kv))]
            inner[head] = jnp.where(kept, piece, inner[head])

    def finish_pair(pair, _):
        @pl.when((me > 0) & (me < n - 1))
        def _():
            for j in range(PAIR):
                head = pair * PAIR + j
                state_copy(head).wait_recv()
                _along, end = log_rows(head)
                decay = jnp.exp(jnp.where(start_last < first, end, -jnp.inf))
                inner[head] = inner[head] + decay * entered[head]
                if pack:
                    @pl.when(me == n - 2)
                    def _():
                        answer(pair, j)
                state_copy(head).start()

        visible = bias[:, 0:rows] == 0.0
        carried = begin[...] < first
        queries = []
        for j in range(PAIR):
            head = pair * PAIR + j
            along, _end = log_rows(head)
            down = along.T
            weight = jnp.exp(jnp.where(visible, down - along, -jnp.inf))
            query = lq[:, lanes(head)]
            scores = against_rows(halves(query), lk[:, lanes(head)]) * weight
            lin[:, lanes(head)] = against_columns(halves(scores), lvh[head])
            reach = jnp.exp(jnp.where(carried, down, -jnp.inf))
            lqh[j] = halves(query * reach)
            reached[j] = reach
            turned = rotated(sq[:, lanes(head)], tab[0, 0:rows, :], tab[1, 0:rows, :]) * scale
            queries.append(halves(turned))
        query = jnp.concatenate(queries, axis=0)
        g = lax.div(pair * PAIR, group)
        width = n * rows
        products = dot(query, keys[g], ((1,), (1,)))
        scores = products[:, :width] + products[:, width:]
        scores = scores + jnp.concatenate([bias[...]] * PAIR, axis=0)
        weights = jnp.exp(scores - jnp.max(scores, axis=1, keepdims=True))
        total = jnp.sum(weights, axis=1, keepdims=True)
        mixed = dot(halves(weights), vals[g], ((1,), (0,)))
        mixed = (mixed[:, :HEAD] + mixed[:, HEAD:]) / total
        for j in range(PAIR):
            sm[:, lanes(pair * PAIR + j)] = mixed[j * rows:(j + 1) * rows]
        out_copy(sm, sm_hbm, sm_sem, pair).start()

        for j in range(PAIR):
            head = pair * PAIR + j
            if n > 1:
                @pl.when((me == n - 1) & (pair >= packed_pairs))
                def _():
                    state_copy(head).wait_recv()

            if pack:
                @pl.when(me == n - 1)
                def _():
                    lin[:, lanes(head)] += reached[j] * entered[head]

                @pl.when(me < n - 1)
                def _():
                    lin[:, lanes(head)] += against_columns(lqh[j], halves(entered[head]))

                attention = lin[:, lanes(head)]
            else:
                attention = lin[:, lanes(head)] + against_columns(lqh[j], halves(entered[head]))
            square = jnp.mean(attention * attention, axis=1, keepdims=True)
            normed = attention * lax.rsqrt(square + EPS) * gain_ref[:, lanes(head)]
            lin[:, lanes(head)] = normed / (1.0 + jnp.exp(-gate[:, lanes(head)]))
        out_copy(lin, lin_hbm, lin_sem, pair).start()
        return 0

    def out_copy(src, dst, sem, pair):
        at = pl.ds(pl.multiple_of(pair * PAIR * HEAD, PAIR * HEAD), PAIR * HEAD)
        return pltpu.make_async_copy(src.at[:, at], dst.at[:, at], sem.at[pair])

    lax.fori_loop(0, pairs, finish_pair, 0)

    def drain(pair, _):
        out_copy(lin, lin_hbm, lin_sem, pair).wait()
        out_copy(sm, sm_hbm, sm_sem, pair).wait()

        @pl.when(me < n - 1)
        def _():
            for j in range(PAIR):
                state_copy(pair * PAIR + j).wait_send()

        if pack:
            @pl.when(me == n - 1)
            def _():
                query_copy(pair).wait_send()

        return 0

    lax.fori_loop(0, pairs, drain, 0)
    for slot in range(n - 1 - pack):
        @pl.when((me < n - 1) & (me >= slot))
        def _():
            kv_copy(slot, 0).wait_send()
            kv_copy(slot, 1).wait_send()


def hand_over(rows, lin_in, sm_in, lin_out, sm_out, held, in_sem, out_sem):
    arrive, leave = [], []
    for part in range(PARTS):
        at = pl.ds(part * (rows // PARTS), rows // PARTS)
        for which, (src, dst) in enumerate([(lin_in, lin_out), (sm_in, sm_out)]):
            slot = held.at[which, at]
            arrive.append(pltpu.make_async_copy(src.at[at], slot, in_sem.at[which, part]))
            leave.append(pltpu.make_async_copy(slot, dst.at[at], out_sem.at[which, part]))
    for copy in arrive:
        copy.start()
    for come, go in zip(arrive, leave):
        come.wait()
        go.start()
    for copy in leave:
        copy.wait()


def shards(
    n, lin_query, lin_key, lin_value, lin_gate, decay_rate, norm_gain, sm_query, sm_key, sm_value, doc_lengths
):
    rows, features = lin_query.shape
    heads, kv = features // HEAD, sm_key.shape[1] // HEAD
    docs = doc_lengths.shape[0]
    pairs = heads // PAIR
    width = n * rows
    anywhere = pl.BlockSpec(memory_space=pl.ANY)
    big = pltpu.VMEM((rows, features), F32)
    table = jnp.asarray(rotary_tables(n, rows))
    out = jax.ShapeDtypeStruct((rows, features), F32)
    call = pl.pallas_call(
        functools.partial(kernel, n, rows, heads, kv, docs),
        out_shape=(out, out),
        in_specs=[pl.BlockSpec(memory_space=pltpu.SMEM)] + [anywhere] * 10,
        out_specs=(anywhere, anywhere),
        scratch_shapes=[
            pltpu.VMEM((heads, rows), F32),
            pltpu.VMEM((1, features), F32),
            pltpu.VMEM((n, 2, rows, kv * HEAD), F32),
            big, big, big, big, big,
            pltpu.VMEM((2, width, HEAD), F32),
            big, big,
            pltpu.VMEM((heads, rows), F32),
            pltpu.VMEM((rows, rows), jnp.int32),
            pltpu.VMEM((rows, width), F32),
            pltpu.VMEM((kv, 2 * width, 2 * HEAD), BF16),
            pltpu.VMEM((kv, 2 * width, 2 * HEAD), BF16),
            pltpu.VMEM((heads, rows, 2 * HEAD), BF16),
            pltpu.VMEM((PAIR, rows, 2 * HEAD), BF16),
            pltpu.VMEM((PAIR, rows, rows), F32),
            big,
            pltpu.VMEM((heads, HEAD, HEAD), F32),
            pltpu.VMEM((heads, HEAD, HEAD), F32),
            pltpu.SemaphoreType.DMA((10,)),
            pltpu.SemaphoreType.DMA((n, 2)),
            pltpu.SemaphoreType.DMA((n, 2)),
            pltpu.SemaphoreType.DMA((heads,)),
            pltpu.SemaphoreType.DMA((heads,)),
            pltpu.SemaphoreType.DMA((pairs,)),
            pltpu.SemaphoreType.DMA((pairs,)),
            pltpu.SemaphoreType.DMA((pairs,)),
            pltpu.SemaphoreType.DMA((pairs,)),
        ],
        compiler_params=pltpu.CompilerParams(
            collective_id=0, has_side_effects=True, vmem_limit_bytes=60 * 1024 * 1024
        ),
    )
    results = call(
        doc_lengths, decay_rate, norm_gain.reshape(1, features), sm_key, sm_value,
        lin_key, lin_value, lin_query, sm_query, lin_gate, table,
    )
    return pl.pallas_call(
        functools.partial(hand_over, rows),
        out_shape=(out, out),
        in_specs=[anywhere] * 2,
        out_specs=(anywhere, anywhere),
        scratch_shapes=[
            pltpu.VMEM((2, rows, features), F32),
            pltpu.SemaphoreType.DMA((2, PARTS)),
            pltpu.SemaphoreType.DMA((2, PARTS)),
        ],
        compiler_params=pltpu.CompilerParams(vmem_limit_bytes=60 * 1024 * 1024),
    )(*results)


def solution(mesh):
    tokens = P(("dp", "context"), "head")
    in_specs = (
        tokens, tokens, tokens, tokens, P("head", ("dp", "context")), P("head"),
        tokens, tokens, tokens, P("dp"),
    )
    return jax.shard_map(
        functools.partial(shards, mesh.shape["context"]),
        mesh=mesh, in_specs=in_specs, out_specs=(tokens, tokens), check_vma=False,
    )
```

```python
import functools

import jax
import jax.numpy as jnp
import numpy as np
from jax import lax
from jax.experimental import pallas as pl
from jax.experimental.pallas import tpu as pltpu
from jax.sharding import PartitionSpec as P

HEAD = 128
ROT = 64
BASE = 10000000.0
EPS = 1e-05
MESH = pl.DeviceIdType.MESH
HIGHEST = lax.Precision.HIGHEST
F32 = jnp.float32
BF16 = jnp.bfloat16
PAIR = 1
PARTS = 4


def rotary_tables(n, rows):
    half = ROT // 2
    exponent = -(2.0 * np.arange(half, dtype=np.float32)) / np.float32(ROT)
    inverse = np.power(np.float32(BASE), exponent.astype(np.float32)).astype(np.float64)
    place = np.arange(rows)[None, :] - rows * np.arange(n)[:, None]
    angle = place.reshape(-1, 1) * inverse[None, :]
    cosine = np.ones((n * rows, HEAD), np.float32)
    sine = np.zeros((n * rows, HEAD), np.float32)
    cosine[:, :half] = cosine[:, half:ROT] = np.cos(angle)
    sine[:, :half] = -np.sin(angle)
    sine[:, half:ROT] = np.sin(angle)
    return np.stack([cosine, sine])


def dot(a, b, contract, precision=None):
    return lax.dot_general(
        a, b, ((contract[0], contract[1]), ((), ())), precision=precision, preferred_element_type=F32
    )


def split(x):
    high = x.astype(BF16)
    return high, (x - high.astype(F32)).astype(BF16)


def halves(x):
    return jnp.concatenate(split(x), axis=1)


def against_rows(lhs, rhs):
    high, low = split(rhs)
    wide = jnp.concatenate(
        [jnp.concatenate([high, high], axis=1), jnp.concatenate([low, low], axis=1)], axis=0
    )
    out = dot(lhs, wide, ((1,), (1,)))
    return out[:, :HEAD] + out[:, HEAD:]


def against_columns(lhs, rhs):
    out = dot(lhs, jnp.concatenate([rhs, rhs], axis=0), ((1,), (0,)))
    return out[:, :HEAD] + out[:, HEAD:]


def rotated(x, cosine, sine):
    half = ROT // 2
    lane = lax.broadcasted_iota(jnp.int32, x.shape, 1)
    swapped = jnp.where(lane < half, pltpu.roll(x, HEAD - half, 1), pltpu.roll(x, half, 1))
    return x * cosine + swapped * sine


def kernel(
    n, rows, heads, kv, docs,
    len_ref, rate_hbm, gain_hbm, sk_hbm, sv_hbm, lk_hbm, lv_hbm, lq_hbm, sq_hbm, gate_hbm, tab_hbm,
    lin_hbm, sm_hbm,
    rate_ref, gain_ref, kvbuf, lk, lv, lq, sq, gate, tab, lin, sm, logd, begin, bias, keys, vals, lvh, lqh, reached, asked, inner, entered,
    load_sem, kv_send, kv_recv, st_send, st_recv, lin_sem, sm_sem, ask_send, ask_recv,
):
    me = lax.axis_index("context")
    first = me * rows
    pairs = heads // PAIR
    group = heads // kv
    right = {"context": me + 1}
    pack = n > 1 and 4 * (n - 1) == 3 * n
    packed_pairs = -(-2 * kv // PAIR) if pack else 0

    barrier = pltpu.get_barrier_semaphore()

    @pl.when(me > 0)
    def _():
        pl.semaphore_signal(barrier, inc=1, device_id={"context": me - 1}, device_id_type=MESH)

    if pack:
        @pl.when(me == n - 2)
        def _():
            pl.semaphore_signal(barrier, inc=1, device_id=right, device_id_type=MESH)

    loads = [
        pltpu.make_async_copy(src, dst, load_sem.at[place])
        for place, (src, dst) in enumerate(
            [
                (rate_hbm, rate_ref), (lk_hbm, lk), (lv_hbm, lv), (sk_hbm, kvbuf.at[0, 0]),
                (sv_hbm, kvbuf.at[0, 1]), (tab_hbm, tab), (lq_hbm, lq), (sq_hbm, sq), (gate_hbm, gate),
                (gain_hbm, gain_ref),
            ]
        )
    ]
    for copy in loads[:3]:
        copy.start()

    def kv_copy(slot, which):
        src = (sk_hbm, sv_hbm)[which] if slot == 0 else kvbuf.at[slot, which]
        return pltpu.make_async_remote_copy(
            src_ref=src, dst_ref=kvbuf.at[slot + 1, which],
            send_sem=kv_send.at[slot, which], recv_sem=kv_recv.at[slot + 1, which],
            device_id=right, device_id_type=MESH,
        )

    def kv_arrival(slot, which):
        return pltpu.make_async_remote_copy(
            src_ref=kvbuf.at[slot, which], dst_ref=kvbuf.at[slot, which],
            send_sem=kv_send.at[slot, which], recv_sem=kv_recv.at[slot, which],
            device_id=right, device_id_type=MESH,
        )

    def state_copy(head):
        return pltpu.make_async_remote_copy(
            src_ref=inner.at[head], dst_ref=entered.at[head],
            send_sem=st_send.at[head], recv_sem=st_recv.at[head],
            device_id=right, device_id_type=MESH,
        )

    def query_copy(pair):
        at = pl.ds(pl.multiple_of(pair * PAIR * HEAD, PAIR * HEAD), PAIR * HEAD)
        return pltpu.make_async_remote_copy(
            src_ref=lq_hbm.at[:, at], dst_ref=asked.at[:, at],
            send_sem=ask_send.at[pair], recv_sem=ask_recv.at[pair],
            device_id={"context": me - 1}, device_id_type=MESH,
        )

    @pl.when(me < n - 1)
    def _():
        pl.semaphore_wait(barrier, 1)
        kv_copy(0, 0).start()
        kv_copy(0, 1).start()

    if pack:
        @pl.when(me == n - 1)
        def _():
            pl.semaphore_wait(barrier, 1)
            for pair in range(pairs):
                query_copy(pair).start()

    for copy in loads[3:]:
        copy.start()

    row = first + lax.broadcasted_iota(jnp.int32, (rows, rows), 0)
    lane = lax.broadcasted_iota(jnp.int32, (rows, rows), 1)
    last = first + rows - 1
    start = jnp.int32(0)
    starts = jnp.zeros((rows, rows), jnp.int32)
    start_last = start_next = jnp.int32(0)
    for d in range(docs):
        starts = jnp.where(row >= start, start, starts)
        start_last = jnp.where(last >= start, start, start_last)
        start_next = jnp.where(last + 1 >= start, start, start_next)
        start = start + len_ref[d]
    begin[...] = starts
    for slot in range(n):
        column = rows * (me - slot) + lane
        bias[:, slot * rows:(slot + 1) * rows] = jnp.where(
            (column >= starts) & (column <= row), 0.0, -jnp.inf
        ).astype(F32)
    upper = jnp.where(
        lax.broadcasted_iota(jnp.int32, (rows, rows), 0) <= lane, 1.0, 0.0
    ).astype(F32)
    loads[0].wait()
    logd[...] = dot(-rate_ref[...], upper, ((1,), (0,)), HIGHEST)

    def lanes(head):
        return pl.ds(pl.multiple_of(head * HEAD, HEAD), HEAD)

    def log_rows(head):
        one = logd[pl.ds(head, 1), :]
        return (
            jnp.broadcast_to(one, (rows, rows)),
            jnp.broadcast_to(one[:, rows - 1:], (rows, rows)),
        )

    loads[1].wait()
    loads[2].wait()
    in_tail = first + lane >= start_last

    def inner_pair(pair, _):
        for j in range(PAIR):
            head = pair * PAIR + j
            along, end = log_rows(head)
            weight = jnp.exp(jnp.where(in_tail, end - along, -jnp.inf))
            turned = lk[:, lanes(head)].T * weight
            both = halves(lv[:, lanes(head)])
            lvh[head] = both
            inner[head] = against_columns(halves(turned), both)

        @pl.when(me == 0)
        def _():
            if n > 1:
                for j in range(PAIR):
                    state_copy(pair * PAIR + j).start()

        return 0

    lax.fori_loop(0, pairs, inner_pair, 0)

    def place_keys(slot, source):
        at = slice(slot * rows, (slot + 1) * rows)
        cosine, sine = tab[0, at, :], tab[1, at, :]
        for g in range(kv):
            high, low = split(rotated(source(0, g), cosine, sine))
            keys[g, at, :] = jnp.concatenate([high, high], axis=1)
            keys[g, n * rows + slot * rows:n * rows + (slot + 1) * rows, :] = jnp.concatenate(
                [low, low], axis=1
            )
            high, low = split(source(1, g))
            both = jnp.concatenate([high, low], axis=1)
            vals[g, at, :] = both
            vals[g, n * rows + slot * rows:n * rows + (slot + 1) * rows, :] = both

    def from_slot(slot):
        return lambda which, g: kvbuf[slot, which, :, g * HEAD:(g + 1) * HEAD]

    def receive(slot):
        @pl.when(me >= slot)
        def _():
            if pack and slot == n - 1:
                for head in range(packed_pairs * PAIR):
                    state_copy(head).wait_recv()
                place_keys(slot, lambda which, g: entered[which * kv + g])
                return
            for which in range(2):
                kv_arrival(slot, which).wait_recv()
                if slot < n - 1 - pack:
                    @pl.when(me < n - 1)
                    def _():
                        kv_copy(slot, which).start()
            place_keys(slot, from_slot(slot))

        @pl.when(me < slot)
        def _():
            for g in range(kv):
                for base in (0, n * rows):
                    at = slice(base + slot * rows, base + (slot + 1) * rows)
                    keys[g, at, :] = jnp.zeros((rows, 2 * HEAD), BF16)
                    vals[g, at, :] = jnp.zeros((rows, 2 * HEAD), BF16)

    for copy in loads[3:6]:
        copy.wait()
    if n > 1:
        receive(1)
    place_keys(0, from_slot(0))
    for slot in range(2, n):
        receive(slot)
    for copy in loads[6:]:
        copy.wait()

    @pl.when(me == 0)
    def _():
        entered[...] = jnp.zeros_like(entered)

    scale = HEAD ** -0.5

    def answer(pair, j):
        if j == 0:
            query_copy(pair).wait_recv()
        kept = row - (n - 2) * rows >= start_next
        head = pair * PAIR + j
        inner[head] = against_columns(halves(asked[:, lanes(head)]), halves(inner[head]))

        @pl.when(head < 2 * kv)
        def _():
            piece = kvbuf[n - 2, lax.div(head, kv), :, lanes(lax.rem(head, kv))]
            inner[head] = jnp.where(kept, piece, inner[head])

    def finish_pair(pair, _):
        @pl.when((me > 0) & (me < n - 1))
        def _():
            for j in range(PAIR):
                head = pair * PAIR + j
                state_copy(head).wait_recv()
                _along, end = log_rows(head)
                decay = jnp.exp(jnp.where(start_last < first, end, -jnp.inf))
                inner[head] = inner[head] + decay * entered[head]
                if pack:
                    @pl.when(me == n - 2)
                    def _():
                        answer(pair, j)
                state_copy(head).start()

        visible = bias[:, 0:rows] == 0.0
        carried = begin[...] < first
        queries = []
        for j in range(PAIR):
            head = pair * PAIR + j
            along, _end = log_rows(head)
            down = along.T
            weight = jnp.exp(jnp.where(visible, down - along, -jnp.inf))
            query = lq[:, lanes(head)]
            scores = against_rows(halves(query), lk[:, lanes(head)]) * weight
            lin[:, lanes(head)] = against_columns(halves(scores), lvh[head])
            reach = jnp.exp(jnp.where(carried, down, -jnp.inf))
            lqh[j] = halves(query * reach)
            reached[j] = reach
            turned = rotated(sq[:, lanes(head)], tab[0, 0:rows, :], tab[1, 0:rows, :]) * scale
            queries.append(halves(turned))
        query = jnp.concatenate(queries, axis=0)
        g = lax.div(pair * PAIR, group)
        width = n * rows
        products = dot(query, keys[g], ((1,), (1,)))
        scores = products[:, :width] + products[:, width:]
        scores = scores + jnp.concatenate([bias[...]] * PAIR, axis=0)
        weights = jnp.exp(scores - jnp.max(scores, axis=1, keepdims=True))
        total = jnp.sum(weights, axis=1, keepdims=True)
        mixed = dot(halves(weights), vals[g], ((1,), (0,)))
        mixed = (mixed[:, :HEAD] + mixed[:, HEAD:]) / total
        for j in range(PAIR):
            sm[:, lanes(pair * PAIR + j)] = mixed[j * rows:(j + 1) * rows]
        out_copy(sm, sm_hbm, sm_sem, pair).start()

        for j in range(PAIR):
            head = pair * PAIR + j
            if n > 1:
                @pl.when((me == n - 1) & (pair >= packed_pairs))
                def _():
                    state_copy(head).wait_recv()

            if pack:
                @pl.when(me == n - 1)
                def _():
                    lin[:, lanes(head)] += reached[j] * entered[head]

                @pl.when(me < n - 1)
                def _():
                    lin[:, lanes(head)] += against_columns(lqh[j], halves(entered[head]))

                attention = lin[:, lanes(head)]
            else:
                attention = lin[:, lanes(head)] + against_columns(lqh[j], halves(entered[head]))
            square = jnp.mean(attention * attention, axis=1, keepdims=True)
            normed = attention * lax.rsqrt(square + EPS) * gain_ref[:, lanes(head)]
            lin[:, lanes(head)] = normed / (1.0 + jnp.exp(-gate[:, lanes(head)]))
        out_copy(lin, lin_hbm, lin_sem, pair).start()
        return 0

    def out_copy(src, dst, sem, pair):
        at = pl.ds(pl.multiple_of(pair * PAIR * HEAD, PAIR * HEAD), PAIR * HEAD)
        return pltpu.make_async_copy(src.at[:, at], dst.at[:, at], sem.at[pair])

    lax.fori_loop(0, pairs, finish_pair, 0)

    def drain(pair, _):
        out_copy(lin, lin_hbm, lin_sem, pair).wait()
        out_copy(sm, sm_hbm, sm_sem, pair).wait()

        @pl.when(me < n - 1)
        def _():
            for j in range(PAIR):
                state_copy(pair * PAIR + j).wait_send()

        if pack:
            @pl.when(me == n - 1)
            def _():
                query_copy(pair).wait_send()

        return 0

    lax.fori_loop(0, pairs, drain, 0)
    for slot in range(n - 1 - pack):
        @pl.when((me < n - 1) & (me >= slot))
        def _():
            kv_copy(slot, 0).wait_send()
            kv_copy(slot, 1).wait_send()


def hand_over(rows, lin_in, sm_in, lin_out, sm_out, held, in_sem, out_sem):
    arrive, leave = [], []
    for part in range(PARTS):
        at = pl.ds(part * (rows // PARTS), rows // PARTS)
        for which, (src, dst) in enumerate([(lin_in, lin_out), (sm_in, sm_out)]):
            slot = held.at[which, at]
            arrive.append(pltpu.make_async_copy(src.at[at], slot, in_sem.at[which, part]))
            leave.append(pltpu.make_async_copy(slot, dst.at[at], out_sem.at[which, part]))
    for copy in arrive:
        copy.start()
    for come, go in zip(arrive, leave):
        come.wait()
        go.start()
    for copy in leave:
        copy.wait()


def shards(
    n, lin_query, lin_key, lin_value, lin_gate, decay_rate, norm_gain, sm_query, sm_key, sm_value, doc_lengths
):
    rows, features = lin_query.shape
    heads, kv = features // HEAD, sm_key.shape[1] // HEAD
    docs = doc_lengths.shape[0]
    pairs = heads // PAIR
    width = n * rows
    anywhere = pl.BlockSpec(memory_space=pl.ANY)
    big = pltpu.VMEM((rows, features), F32)
    table = jnp.asarray(rotary_tables(n, rows))
    out = jax.ShapeDtypeStruct((rows, features), F32)
    call = pl.pallas_call(
        functools.partial(kernel, n, rows, heads, kv, docs),
        out_shape=(out, out),
        in_specs=[pl.BlockSpec(memory_space=pltpu.SMEM)] + [anywhere] * 10,
        out_specs=(anywhere, anywhere),
        scratch_shapes=[
            pltpu.VMEM((heads, rows), F32),
            pltpu.VMEM((1, features), F32),
            pltpu.VMEM((n, 2, rows, kv * HEAD), F32),
            big, big, big, big, big,
            pltpu.VMEM((2, width, HEAD), F32),
            big, big,
            pltpu.VMEM((heads, rows), F32),
            pltpu.VMEM((rows, rows), jnp.int32),
            pltpu.VMEM((rows, width), F32),
            pltpu.VMEM((kv, 2 * width, 2 * HEAD), BF16),
            pltpu.VMEM((kv, 2 * width, 2 * HEAD), BF16),
            pltpu.VMEM((heads, rows, 2 * HEAD), BF16),
            pltpu.VMEM((PAIR, rows, 2 * HEAD), BF16),
            pltpu.VMEM((PAIR, rows, rows), F32),
            big,
            pltpu.VMEM((heads, HEAD, HEAD), F32),
            pltpu.VMEM((heads, HEAD, HEAD), F32),
            pltpu.SemaphoreType.DMA((10,)),
            pltpu.SemaphoreType.DMA((n, 2)),
            pltpu.SemaphoreType.DMA((n, 2)),
            pltpu.SemaphoreType.DMA((heads,)),
            pltpu.SemaphoreType.DMA((heads,)),
            pltpu.SemaphoreType.DMA((pairs,)),
            pltpu.SemaphoreType.DMA((pairs,)),
            pltpu.SemaphoreType.DMA((pairs,)),
            pltpu.SemaphoreType.DMA((pairs,)),
        ],
        compiler_params=pltpu.CompilerParams(
            collective_id=0, has_side_effects=True, vmem_limit_bytes=60 * 1024 * 1024
        ),
    )
    results = call(
        doc_lengths, decay_rate, norm_gain.reshape(1, features), sm_key, sm_value,
        lin_key, lin_value, lin_query, sm_query, lin_gate, table,
    )
    return pl.pallas_call(
        functools.partial(hand_over, rows),
        out_shape=(out, out),
        in_specs=[anywhere] * 2,
        out_specs=(anywhere, anywhere),
        scratch_shapes=[
            pltpu.VMEM((2, rows, features), F32),
            pltpu.SemaphoreType.DMA((2, PARTS)),
            pltpu.SemaphoreType.DMA((2, PARTS)),
        ],
        compiler_params=pltpu.CompilerParams(vmem_limit_bytes=60 * 1024 * 1024),
    )(*results)


def solution(mesh):
    tokens = P(("dp", "context"), "head")
    in_specs = (
        tokens, tokens, tokens, tokens, P("head", ("dp", "context")), P("head"),
        tokens, tokens, tokens, P("dp"),
    )
    return jax.shard_map(
        functools.partial(shards, mesh.shape["context"]),
        mesh=mesh, in_specs=in_specs, out_specs=(tokens, tokens), check_vma=False,
    )
```
